256 devices in a mesh: dp: 8 (over z), seq: 32 (over y, x, core).
Axes of the slice: x: 4, y: 4, z: 8, core: 2. Of those that a mesh axis runs over, the one named last changes fastest.
Arguments:
- tokens: bfloat16 [8, 16384, 1024], P('dp', 'seq'), may hold values from -6 to 6
- grad_out: bfloat16 [8, 16384, 1024], P('dp', 'seq'), may hold values from -6 to 6
- src_order: int32 [32, 32], P('seq'), may hold values from 0 to 31, each once within a row
- dst_order: int32 [32, 32], P('seq'), may hold values from 0 to 31, each once within a row
- w_proj: bfloat16 [1024, 1152], replicated, may hold values from -0.0234375 to 0.0234375
- w_dt: bfloat16 [1024, 16], replicated, may hold values from -0.1875 to 0.1875
- w_out: bfloat16 [1024, 1024], replicated, may hold values from -0.1875 to 0.1875
- dt_bias: float32 [16], replicated, may hold values from -0.5 to 1
- decay_rate: float32 [16], replicated, may hold values from 1.2207031e-05 to 0.04, as said below
- d_skip: float32 [16], replicated, may hold values from 0.5 to 2
- norm_gain: float32 [1024], replicated, may hold values from 0.5 to 1.5
Outputs:
- grad_tokens: bfloat16 [8, 16384, 1024], P('dp', 'seq')
- grad_w_proj: float32 [1024, 1152], P('seq')
- grad_w_dt: float32 [1024, 16], P('seq')
- grad_w_out: float32 [1024, 1024], P(None, 'seq')
The draws below stay inside these ranges and needn't reach their ends.
Inputs may be any that keep to these rules, and one draw needn't show every extreme that they name: `src_order`: each row is a permutation of 0 to 31. `dst_order`: each row is a permutation of 0 to 31. `decay_rate`: positive rates.
All inputs are finite; a program needn't handle non-finite values.
Results may differ from the reference program's by a relative error of at most 0.005.
Values may be sent and summed in bfloat16 or wider, within the bound.
A program may use at most 192 MiB of HBM per device.

```python
import math
import jax
import jax.numpy as jnp
from jax import lax

D = 1024
H = 16
P_SIZE = 64
N = 64
SPAN = 256
BLK = 16
CLIPS = 8
SEQ_LEN = 16384
NB_DEV = 32
PROJ = 1152
N_SEQ = 32


def draw_decay_rate(key, part):
    key = jax.random.fold_in(key, 11)
    pick, slow_key, fast_key = jax.random.split(key, 3)
    share = 0.5
    length = 1.0 * SEQ_LEN
    slow = jax.random.uniform(slow_key, (H,), minval=math.log(0.2 / length), maxval=math.log(2.0 / length))
    fast = jax.random.uniform(fast_key, (H,), minval=math.log(2.0 / length), maxval=math.log(1.0 / 25.0))
    chosen = jax.random.uniform(pick, (H,)) < share
    return jnp.exp(jnp.where(chosen, slow, fast)).astype(jnp.float32)


def spiked(drawn, stream_key, source, target, shards_of, factor):
    owner, partner = [(jnp.arange(drawn.shape[position]) // (drawn.shape[position] // shards_of)).reshape([-1 if axis == position else 1 for axis in range(drawn.ndim)]) for position in (source, target)]
    chosen = jax.random.permutation(stream_key, shards_of)[partner]
    strong = (owner == chosen) | (owner == (partner + shards_of // 2) % shards_of)
    return jnp.where(strong, factor * drawn, drawn)


def steps_of(key, shape, cuts, low, top_value):
    loudness = 1.0
    for axis_at, blocks in cuts:
        heights = jax.random.uniform(jax.random.fold_in(jax.random.fold_in(key, 6), axis_at), (blocks,), jnp.float32, low / len(cuts), top_value / len(cuts))
        loudness = loudness * jnp.repeat(jnp.exp(heights), shape[axis_at] // blocks).reshape((-1,) + (1,) * (len(shape) - 1 - axis_at))
    return loudness


def centred(key, shape, deviation, bound, shards=(), kind=jnp.bfloat16):
    factor_of = steps_of(key, shape, shards, -0.22, 0.18) if shards else 1.0
    values = jax.random.normal(key, shape, jnp.float32) * deviation * factor_of
    return jnp.minimum(jnp.maximum(values, -bound), bound).astype(kind)


def bell_draw_with(own_key, dims, scale, limit, shards, heavy, held_as=jnp.bfloat16):
    result = scale * jax.random.normal(own_key, dims, jnp.float32)
    if shards:
        result = result * steps_of(own_key, dims, shards, -0.22, 0.18)
    return jnp.clip(spiked(result, jax.random.fold_in(own_key, 3), *heavy), -limit, limit).astype(held_as)


def setup_inputs(seed: int = 0) -> dict:
    key_of = jax.random.split(jax.random.key(seed), 12)
    return {
        "tokens": bell_draw_with(key_of[0], (CLIPS, SEQ_LEN, D), 1.0, 6.0, ((0, 8), (1, 32)), (1, 2, 32, 2.75)),
        "grad_out": bell_draw_with(key_of[1], (CLIPS, SEQ_LEN, D), 1.0, 6.0, ((0, 8), (1, 32)), (1, 2, 32, 2.75)),
        "src_order": jax.vmap(lambda own: jax.random.permutation(own, NB_DEV))(jax.random.split(key_of[2], N_SEQ)).reshape((N_SEQ, NB_DEV)).astype(jnp.int32),
        "dst_order": jax.vmap(lambda own: jax.random.permutation(own, NB_DEV))(jax.random.split(key_of[3], N_SEQ)).reshape((N_SEQ, NB_DEV)).astype(jnp.int32),
        "w_proj": centred(key_of[4], (D, PROJ), (64 * D) ** -0.5, 0.0234375),
        "w_dt": centred(key_of[5], (D, H), D ** -0.5, 0.1875),
        "w_out": centred(key_of[6], (H * P_SIZE, D), (H * P_SIZE) ** -0.5, 0.1875),
        "dt_bias": jnp.clip(jax.random.uniform(key_of[7], (H,), jnp.float32, -0.5, 1.0), -0.5, 1.0),
        "decay_rate": draw_decay_rate(jax.random.fold_in(key_of[11], 71), 0),
        "d_skip": jnp.clip(jax.random.uniform(key_of[9], (H,), jnp.float32, 0.5, 2.0), 0.5, 2.0),
        "norm_gain": jnp.clip(jax.random.uniform(key_of[10], (H * P_SIZE,), jnp.float32, 0.5, 1.5), 0.5, 1.5),
    }


HIGHEST = lax.Precision.HIGHEST
EPSILON = 1e-05

def span_step(state, block):
    values, delta, decay_log, inject, readout = block
    running = jnp.cumsum(decay_log, axis=0)
    length = running.shape[0]
    lower = jnp.arange(length)[:, None] >= jnp.arange(length)[None, :]
    spread = running.T[:, :, None] - running.T[:, None, :]
    decay = jnp.exp(jnp.where(lower[None, :, :], spread, -jnp.inf))
    scores = jnp.dot(readout, inject.T, precision=HIGHEST)
    mixing = decay * scores[None, :, :] * delta.T[:, None, :]
    inside = jnp.einsum('hts,shp->thp', mixing, values, precision=HIGHEST)
    carried = jnp.einsum('tn,hpn->thp', readout, state, precision=HIGHEST) * jnp.exp(running)[:, :, None]
    total = running[-1]
    weight = jnp.exp(total[None, :] - running) * delta
    added = jnp.einsum('thp,tn->hpn', values * weight[:, :, None], inject, precision=HIGHEST)
    return (jnp.exp(total)[:, None, None] * state + added, inside + carried)

def ssd_scan(values, delta_raw, inject_read, start, dt_bias, decay_rate):
    count = values.shape[0]
    blocks = count // SPAN
    delta = jax.nn.softplus(delta_raw + dt_bias[None, :])
    decay_log = -decay_rate[None, :] * delta
    pieces = (values.reshape(blocks, SPAN, H, P_SIZE), delta.reshape(blocks, SPAN, H), decay_log.reshape(blocks, SPAN, H), inject_read[:, :N].reshape(blocks, SPAN, N), inject_read[:, N:].reshape(blocks, SPAN, N))
    final, outputs = lax.scan(span_step, start, pieces)
    return (outputs.reshape(count, H * P_SIZE), final)

def finish(mixed, values, d_skip, norm_gain):
    count = mixed.shape[0]
    summed = (mixed + jnp.repeat(d_skip, P_SIZE)[None, :] * values).reshape(count, H, P_SIZE)
    scale = lax.rsqrt(lax.optimization_barrier(jnp.mean(summed * summed, axis=2, keepdims=True)) + EPSILON)
    return (summed * scale).reshape(count, H * P_SIZE) * norm_gain[None, :]

def to_scan(array, src_order, dst_order):
    width = array.shape[-1]
    blocks = array.reshape(N_SEQ, NB_DEV, BLK, width)
    blocks = jnp.take_along_axis(blocks, src_order[:, :, None, None], axis=1)
    blocks = blocks.reshape(N_SEQ, N_SEQ, NB_DEV // N_SEQ, BLK, width).transpose(1, 0, 2, 3, 4)
    blocks = blocks.reshape(N_SEQ, NB_DEV, BLK, width)
    blocks = jnp.take_along_axis(blocks, dst_order[:, :, None, None], axis=1)
    return blocks.reshape(N_SEQ * NB_DEV * BLK, width)

def from_scan(array, src_order, dst_order):
    width = array.shape[-1]
    inverse_src = jnp.argsort(src_order, axis=1).astype(jnp.int32)
    inverse_dst = jnp.argsort(dst_order, axis=1).astype(jnp.int32)
    blocks = array.reshape(N_SEQ, NB_DEV, BLK, width)
    blocks = jnp.take_along_axis(blocks, inverse_dst[:, :, None, None], axis=1)
    blocks = blocks.reshape(N_SEQ, N_SEQ, NB_DEV // N_SEQ, BLK, width).transpose(1, 0, 2, 3, 4)
    blocks = blocks.reshape(N_SEQ, NB_DEV, BLK, width)
    blocks = jnp.take_along_axis(blocks, inverse_src[:, :, None, None], axis=1)
    return blocks.reshape(N_SEQ * NB_DEV * BLK, width)

def reference(tokens, grad_out, src_order, dst_order, w_proj, w_dt, w_out, dt_bias, decay_rate, d_skip, norm_gain):
    inner = H * P_SIZE

    def one_clip(pair):
        clip_tokens, clip_grads = pair
        scan_tokens = to_scan(clip_tokens, src_order, dst_order)
        scan_grads = to_scan(clip_grads, src_order, dst_order)
        projected = jnp.dot(scan_tokens, w_proj, preferred_element_type=jnp.float32)
        delta_raw = jnp.dot(scan_tokens, w_dt, preferred_element_type=jnp.float32)
        values = projected[:, :inner]
        inject_read = projected[:, inner:]

        def forward(values, delta_raw, inject_read):
            start = jnp.zeros((H, P_SIZE, N), jnp.float32)
            mixed, final = ssd_scan(values, delta_raw, inject_read, start, dt_bias, decay_rate)
            return finish(mixed, values, d_skip, norm_gain)
        normed, backward = jax.vjp(forward, values, delta_raw, inject_read)
        grad_normed = jnp.dot(scan_grads, w_out.T, preferred_element_type=jnp.float32)
        grad_values, grad_delta, grad_inject = backward(grad_normed)
        grad_proj = jnp.concatenate([grad_values, grad_inject], axis=1).astype(jnp.bfloat16)
        grad_delta_low = grad_delta.astype(jnp.bfloat16)
        grad_scan = (jnp.dot(grad_proj, w_proj.T, preferred_element_type=jnp.float32) + jnp.dot(grad_delta_low, w_dt.T, preferred_element_type=jnp.float32)).astype(jnp.bfloat16)
        normed_low = normed.astype(jnp.bfloat16)
        return (from_scan(grad_scan, src_order, dst_order), jnp.dot(scan_tokens.T, grad_proj, preferred_element_type=jnp.float32), jnp.dot(scan_tokens.T, grad_delta_low, preferred_element_type=jnp.float32), jnp.dot(normed_low.T, scan_grads, preferred_element_type=jnp.float32))
    grad_tokens, proj_terms, delta_terms, out_terms = lax.map(one_clip, (tokens, grad_out))
    scale = (CLIPS * SEQ_LEN) ** (-0.5)
    return (grad_tokens, lax.optimization_barrier(jnp.sum(proj_terms, axis=0)) * scale, lax.optimization_barrier(jnp.sum(delta_terms, axis=0)) * scale, lax.optimization_barrier(jnp.sum(out_terms, axis=0)) * scale)
```

```python
import functools

import jax
import jax.numpy as jnp
from jax import lax
from jax.experimental import pallas as pl
from jax.experimental.pallas import tpu as pltpu
from jax.sharding import PartitionSpec as P

H = 16
P_SIZE = 64
N = 64
D = 1024
PROJ = 1152
BLK = 16
NSEQ = 32
NDP = 8
T = 512
L = 128
NC = T // L
EPSILON = 1e-05
F32 = jnp.float32
BF16 = jnp.bfloat16
MESH = pl.DeviceIdType.MESH
VMEM_LIMIT = 48 * 1024 * 1024

VM = pl.BlockSpec(memory_space=pltpu.VMEM)
SM = pl.BlockSpec(memory_space=pltpu.SMEM)

NN = (((1,), (0,)), ((), ()))
NT = (((1,), (1,)), ((), ()))
TN = (((0,), (0,)), ((), ()))


def dot(a, b, dims=NN):
    return lax.dot_general(a, b, dims, preferred_element_type=F32)


def split2(a):
    hi = a.astype(BF16)
    return hi, (a - hi.astype(F32)).astype(BF16)


def split3(a):
    hi, mid = split2(a)
    low = a - hi.astype(F32) - mid.astype(F32)
    return hi, mid, low.astype(BF16)


def dot_exact_right(a, b, dims=NN):
    hi, lo = split2(a)
    return dot(hi, b, dims) + dot(lo, b, dims)


def dot_exact_left3(a, b):
    hi, mid, low = split3(b)
    return (dot(a, low) + dot(a, mid)) + dot(a, hi)


def wide_dot(a, b, dims=NN):
    ka, kb = dims[0][0][0], dims[0][1][0]
    ah, al = split2(a)
    bh, bl = split2(b)
    return dot(
        jnp.concatenate([ah, al, ah], axis=ka), jnp.concatenate([bh, bh, bl], axis=kb), dims
    )


def three_dots(a, b, dims=NN):
    ah, al = split2(a)
    bh, bl = split2(b)
    return (dot(al, bh, dims) + dot(ah, bl, dims)) + dot(ah, bh, dims)


def iota(shape, dim):
    return lax.broadcasted_iota(jnp.int32, shape, dim)


def head_rows():
    return ((iota((H, D), 1) >> 6) == iota((H, D), 0)).astype(F32).astype(BF16)


def head_columns():
    return ((iota((D, H), 0) >> 6) == iota((D, H), 1)).astype(F32).astype(BF16)


def lower_ones():
    return (iota((L, L), 0) >= iota((L, L), 1)).astype(F32).astype(BF16)


def upper_ones():
    return (iota((L, L), 0) <= iota((L, L), 1)).astype(F32).astype(BF16)


def softplus(v):
    return jnp.maximum(v, 0.0) + jnp.log1p(jnp.exp(-jnp.abs(v)))


def sigmoid(v):
    e = jnp.exp(-jnp.abs(v))
    return jnp.where(v >= 0, 1.0, e) / (1.0 + e)


def ids(k):
    z = lax.axis_index("dp")
    me = lax.axis_index("seq")
    return z, me, lax.rem(me + k, NSEQ), lax.rem(me - k + NSEQ, NSEQ)


def greet_all():
    z = lax.axis_index("dp")
    me = lax.axis_index("seq")
    barrier = pltpu.get_barrier_semaphore()

    def hello(k, _):
        pl.semaphore_signal(
            barrier, inc=1, device_id=(z, lax.rem(me + k, NSEQ)), device_id_type=MESH
        )
        return 0

    lax.fori_loop(1, NSEQ, hello, 0)
    pl.semaphore_wait(barrier, NSEQ - 1)


def to_peer(src, dst, send_sem, recv_sem, peer):
    return pltpu.make_async_remote_copy(
        src_ref=src, dst_ref=dst, send_sem=send_sem, recv_sem=recv_sem,
        device_id=peer, device_id_type=MESH,
    )


def scatter_blocks(send, recv, send_sem, recv_sem):
    me = lax.axis_index("seq")

    def go(k, _):
        z, _, to, _ = ids(k)
        to_peer(send.at[to], recv.at[me], send_sem.at[to], recv_sem.at[me], (z, to)).start()
        return 0

    lax.fori_loop(1, NSEQ, go, 0)


def await_blocks(send, recv, send_sem, recv_sem):
    def done(k, _):
        z, _, to, frm = ids(k)
        copy = to_peer(send.at[to], recv.at[frm], send_sem.at[to], recv_sem.at[frm], (z, to))
        copy.wait_send()
        copy.wait_recv()
        return 0

    lax.fori_loop(1, NSEQ, done, 0)


def enter_kernel(src_ref, dst_ref, tok_ref, grad_ref, x_ref, g_ref,
                 send_t, send_g, recv_t, recv_g, st, rt, sg, rg):
    me = lax.axis_index("seq")

    def load_t(d, _):
        send_t[d] = tok_ref[src_ref[0, d]]
        return 0

    def load_g(d, _):
        send_g[d] = grad_ref[src_ref[0, d]]
        return 0

    lax.fori_loop(0, NSEQ, load_t, 0)
    greet_all()
    scatter_blocks(send_t, recv_t, st, rt)
    lax.fori_loop(0, NSEQ, load_g, 0)
    scatter_blocks(send_g, recv_g, sg, rg)
    recv_t[me] = send_t[me]
    recv_g[me] = send_g[me]
    await_blocks(send_t, recv_t, st, rt)

    def settle_t(j, _):
        x_ref[j] = recv_t[dst_ref[0, j]]
        return 0

    lax.fori_loop(0, NSEQ, settle_t, 0)
    await_blocks(send_g, recv_g, sg, rg)

    def settle_g(j, _):
        g_ref[j] = recv_g[dst_ref[0, j]]
        return 0

    lax.fori_loop(0, NSEQ, settle_g, 0)


def enter(tokens, grads, src, dst):
    shape = (NSEQ, BLK, D)
    block = pltpu.VMEM(shape, BF16)
    sems = pltpu.SemaphoreType.DMA((NSEQ,))
    return pl.pallas_call(
        enter_kernel,
        out_shape=[jax.ShapeDtypeStruct(shape, BF16)] * 2,
        in_specs=[SM, SM, VM, VM],
        out_specs=[VM, VM],
        scratch_shapes=[block] * 4 + [sems] * 4,
        compiler_params=pltpu.CompilerParams(
            collective_id=0, has_side_effects=True, vmem_limit_bytes=VMEM_LIMIT
        ),
        name="enter",
    )(src, dst, tokens, grads)


def leave_kernel(inv_ref, ret_ref, out_ref, recv, ss, rs):
    me = lax.axis_index("seq")
    greet_all()
    scatter_blocks(ret_ref, recv, ss, rs)
    recv[me] = ret_ref[me]
    await_blocks(ret_ref, recv, ss, rs)

    def settle(j, _):
        out_ref[j] = recv[inv_ref[0, j]]
        return 0

    lax.fori_loop(0, NSEQ, settle, 0)


def leave(inverse, returning):
    shape = (NSEQ, BLK, D)
    sems = pltpu.SemaphoreType.DMA((NSEQ,))
    return pl.pallas_call(
        leave_kernel,
        out_shape=jax.ShapeDtypeStruct(shape, BF16),
        in_specs=[SM, VM],
        out_specs=VM,
        scratch_shapes=[pltpu.VMEM(shape, BF16), sems, sems],
        compiler_params=pltpu.CompilerParams(
            collective_id=1, has_side_effects=True, vmem_limit_bytes=VMEM_LIMIT
        ),
        name="leave",
    )(inverse, returning)


def relay_kernel(reverse, pay_ref, out_ref, recv, mid, s1, r1, s2, r2):
    me = lax.axis_index("seq")
    greet_all()
    scatter_blocks(pay_ref, recv, s1, r1)
    recv[me] = pay_ref[me]
    await_blocks(pay_ref, recv, s1, r1)

    def step(i, state):
        j = NSEQ - 1 - i if reverse else i
        mid[j] = state
        return recv[j, 8:16] * state + recv[j, 0:8]

    lax.fori_loop(0, NSEQ, step, jnp.zeros((8, 256), F32))
    scatter_blocks(mid, out_ref, s2, r2)
    out_ref[me] = mid[me]
    await_blocks(mid, out_ref, s2, r2)


def relay(payload, reverse):
    sems = pltpu.SemaphoreType.DMA((NSEQ,))
    shape = (NSEQ, 8, 256)
    return pl.pallas_call(
        functools.partial(relay_kernel, reverse),
        out_shape=jax.ShapeDtypeStruct(shape, F32),
        in_specs=[VM],
        out_specs=VM,
        scratch_shapes=[
            pltpu.VMEM((NSEQ, 16, 256), F32), pltpu.VMEM(shape, F32), sems, sems, sems, sems
        ],
        compiler_params=pltpu.CompilerParams(
            collective_id=3 if reverse else 2, has_side_effects=True,
            vmem_limit_bytes=VMEM_LIMIT,
        ),
        name="relay_back" if reverse else "relay",
    )(payload)


def pack_payload(pay_ref, state, keep):
    for rg in range(8):
        for lg in range(4):
            lanes = slice(256 * lg, 256 * lg + 256)
            pay_ref[rg * 4 + lg, 0:8, :] = state[8 * rg:8 * rg + 8, lanes]
            pay_ref[rg * 4 + lg, 8:16, :] = jnp.broadcast_to(keep[:, lanes], (8, 256))


def unpack_state(ref, state_ref):
    for rg in range(8):
        for lg in range(4):
            state_ref[8 * rg:8 * rg + 8, 256 * lg:256 * lg + 256] = ref[rg * 4 + lg]


def project_kernel(x_ref, wp_ref, wd_ref, bias_ref, rate_ref,
                   v_ref, bc_ref, raw_ref, run_ref, runt_ref, u_ref, pay_ref):
    heads = head_rows()
    lower = lower_ones()
    bias = bias_ref[...]
    rate = rate_ref[...]

    def chunk(c, carry):
        state, total = carry
        rows = pl.ds(pl.multiple_of(c * L, L), L)
        x = x_ref[rows, :]
        v = dot(x, wp_ref[:, 0:D])
        v_ref[rows, :] = v
        bc = dot(x, wp_ref[:, D:PROJ])
        bc_ref[rows, :] = bc
        raw = dot(x, wd_ref[...]) + bias
        raw_ref[rows, :] = raw
        delta = softplus(raw)
        running = dot_exact_left3(lower, -rate * delta)
        run_ref[rows, :] = running
        runt_ref[c] = running.T
        last = running[L - 1:L, :]
        weight = jnp.exp(last - running) * delta
        weighted = v * dot_exact_right(weight, heads)
        added = wide_dot(bc[:, 0:N], weighted, TN)
        u_ref[c] = added
        keep = dot_exact_right(jnp.broadcast_to(jnp.exp(last), (8, H)), heads)[0:1]
        return keep * state + added, total + last

    state, total = lax.fori_loop(
        0, NC, chunk, (jnp.zeros((N, D), F32), jnp.zeros((1, H), F32))
    )
    hi, mid, low = split3(jnp.broadcast_to(jnp.exp(total), (8, H)))
    keep = (dot(low, heads) + dot(mid, heads)) + dot(hi, heads)
    pack_payload(pay_ref, state, keep[0:1])


def project(x, w_proj, w_dt, bias, rate):
    return pl.pallas_call(
        project_kernel,
        out_shape=[
            jax.ShapeDtypeStruct((T, D), F32),
            jax.ShapeDtypeStruct((T, 2 * N), F32),
            jax.ShapeDtypeStruct((T, H), F32),
            jax.ShapeDtypeStruct((T, H), F32),
            jax.ShapeDtypeStruct((NC, H, L), F32),
            jax.ShapeDtypeStruct((NC, N, D), F32),
            jax.ShapeDtypeStruct((NSEQ, 16, 256), F32),
        ],
        in_specs=[VM] * 5,
        out_specs=[VM] * 7,
        compiler_params=pltpu.CompilerParams(vmem_limit_bytes=VMEM_LIMIT),
        name="project",
    )(x, w_proj, w_dt, bias, rate)


def forward_kernel(ent_ref, v_ref, bc_ref, raw_ref, run_ref, runt_ref, u_ref, g_ref, wo_ref,
                   skip_ref, gain_ref,
                   dy_ref, low_ref, q_ref, dc_ref, s_ref, r_ref, pay_ref, state_ref):
    heads = head_rows()
    cols = head_columns()
    lanes = iota((1, 128), 1)
    even = lanes < 64
    skip = dot_exact_right(jnp.broadcast_to(skip_ref[...], (8, H)), heads)[0:1]
    gain = gain_ref[...]
    unpack_state(ent_ref, state_ref)
    below = iota((L, L), 0) >= iota((L, L), 1)

    def chunk(c, carry):
        out_grad, before, total = carry
        rows = pl.ds(pl.multiple_of(c * L, L), L)
        v = v_ref[rows, :]
        bc = bc_ref[rows, :]
        b, r = bc[:, 0:N], bc[:, N:2 * N]
        delta = softplus(raw_ref[rows, :])
        running = run_ref[rows, :]
        runt = runt_ref[c]
        last = running[L - 1:L, :]
        state = state_ref[...]
        s_ref[c] = state
        grown = dot_exact_right(jnp.exp(running), heads)
        carried = wide_dot(r, state) * grown
        scaled = (v * dot_exact_right(delta, heads)).astype(BF16)
        scores = wide_dot(r, b, NT)
        inside = []
        for j in range(H // 2):
            mixes = []
            for h in (2 * j, 2 * j + 1):
                spread = running[:, h:h + 1] - runt[h:h + 1, :]
                decay = jnp.exp(jnp.where(below, spread, -jnp.inf))
                mixes.append((decay * scores).astype(BF16))
            pair = scaled[:, 128 * j:128 * j + 128]
            zero = jnp.zeros_like(pair)
            stacked = jnp.concatenate(
                [jnp.where(even, pair, zero), jnp.where(even, zero, pair)], axis=0
            )
            inside.append(dot(jnp.concatenate(mixes, axis=1), stacked))
        summed = jnp.concatenate(inside, axis=1) + carried + skip * v
        square = dot_exact_right(summed * summed, cols) * (1.0 / P_SIZE)
        scale = dot_exact_right(lax.rsqrt(square + EPSILON), heads)
        unit = summed * scale
        low_ref[rows, :] = (unit * gain).astype(BF16)
        grad_unit = dot(g_ref[rows, :], wo_ref[...], NT) * gain
        along = dot_exact_right(grad_unit * unit, cols) * (1.0 / P_SIZE)
        dy = scale * (grad_unit - unit * dot_exact_right(along, heads))
        dy_ref[rows, :] = dy
        q_ref[rows, :] = dot_exact_right(dy * carried, cols)
        back = dy * grown
        dc_ref[rows, :] = three_dots(back, state, NT)
        reach = wide_dot(r, back, TN)
        r_ref[c] = reach
        keep = dot_exact_right(jnp.broadcast_to(jnp.exp(last), (8, H)), heads)[0:1]
        state_ref[...] = keep * state + u_ref[c]
        return out_grad + before * reach, before * keep, total + last

    out_grad, _, total = lax.fori_loop(
        0, NC, chunk,
        (jnp.zeros((N, D), F32), jnp.ones((1, D), F32), jnp.zeros((1, H), F32)),
    )
    hi, mid, low = split3(jnp.broadcast_to(jnp.exp(total), (8, H)))
    keep = (dot(low, heads) + dot(mid, heads)) + dot(hi, heads)
    pack_payload(pay_ref, out_grad, keep[0:1])


def forward(entering, v, bc, raw, run, runt, u, g, w_out, skip, gain):
    return pl.pallas_call(
        forward_kernel,
        out_shape=[
            jax.ShapeDtypeStruct((T, D), F32),
            jax.ShapeDtypeStruct((T, D), BF16),
            jax.ShapeDtypeStruct((T, H), F32),
            jax.ShapeDtypeStruct((T, N), F32),
            jax.ShapeDtypeStruct((NC, N, D), F32),
            jax.ShapeDtypeStruct((NC, N, D), F32),
            jax.ShapeDtypeStruct((NSEQ, 16, 256), F32),
        ],
        in_specs=[VM] * 11,
        out_specs=[VM] * 7,
        scratch_shapes=[pltpu.VMEM((N, D), F32)],
        compiler_params=pltpu.CompilerParams(vmem_limit_bytes=VMEM_LIMIT),
        name="forward",
    )(entering, v, bc, raw, run, runt, u, g, w_out, skip, gain)


def backward_kernel(src_ref, dst_ref, lv_ref, x_ref, g_ref, v_ref, bc_ref, raw_ref, run_ref,
                    runt_ref, dy_ref, low_ref, q_ref, dc_ref, s_ref, r_ref,
                    wp_ref, wd_ref, rate_ref, skip_ref,
                    ret_ref, inv_ref, p1_ref, p2_ref,
                    grad_ref, gp_ref, gd_ref):
    heads = head_rows()
    cols = head_columns()
    upper = upper_ones()
    even = iota((1, 128), 1) < 64
    skip = dot_exact_right(jnp.broadcast_to(skip_ref[...], (8, H)), heads)[0:1]
    rate = rate_ref[...]
    unpack_state(lv_ref, grad_ref)
    after = iota((L, L), 1) >= iota((L, L), 0)
    half = iota((2 * L, H), 0) >> 7
    pick = iota((2 * L, H), 1)
    halft = iota((H, 2 * L), 1) >> 7
    pickt = iota((H, 2 * L), 0)

    def invert(d, _):
        inv_ref[0, src_ref[0, d]] = d
        return 0

    lax.fori_loop(0, NSEQ, invert, 0)

    def chunk(i, _):
        c = NC - 1 - i
        rows = pl.ds(pl.multiple_of(c * L, L), L)
        v = v_ref[rows, :]
        bc = bc_ref[rows, :]
        b, r = bc[:, 0:N], bc[:, N:2 * N]
        raw = raw_ref[rows, :]
        delta = softplus(raw)
        running = run_ref[rows, :]
        runt = runt_ref[c]
        last = running[L - 1:L, :]
        dy = dy_ref[rows, :]
        dy_low = dy.astype(BF16)
        grad = grad_ref[...]
        widened = dot_exact_right(delta, heads)
        scaled = v * widened
        scaled_low = scaled.astype(BF16)
        fade = dot_exact_right(jnp.exp(last - running), heads)
        weighted = scaled * fade
        d_weighted = wide_dot(b, grad)
        used = dot_exact_right(d_weighted * weighted, cols)
        db = three_dots(weighted, grad, NT)
        keep = dot_exact_right(jnp.broadcast_to(jnp.exp(last), (8, H)), heads)[0:1]
        held = jnp.sum(keep * grad * s_ref[c], axis=0, keepdims=True)
        held = dot_exact_right(jnp.broadcast_to(held, (8, D)), cols)[0:1]
        scores_t = wide_dot(b, r, NT)
        dscores_t = jnp.zeros((L, L), F32)
        by_source = jnp.zeros((L, H), F32)
        by_target = jnp.zeros((H, L), F32)
        inside = []
        for j in range(H // 2):
            pair = slice(128 * j, 128 * j + 128)
            sp = scaled_low[:, pair]
            dp = dy_low[:, pair]
            zero = jnp.zeros_like(sp)
            mixes, flows = [], []
            for e in (0, 1):
                h = 2 * j + e
                spread = runt[h:h + 1, :] - running[:, h:h + 1]
                decay = jnp.exp(jnp.where(after, spread, -jnp.inf))
                mixes.append((decay * scores_t).astype(BF16))
                mine = jnp.where(even, sp, zero) if e == 0 else jnp.where(even, zero, sp)
                moved = dot(mine, dp, NT) * decay
                dscores_t = dscores_t + moved
                flows.append((moved * scores_t).astype(BF16))
            stacked = jnp.concatenate(
                [jnp.where(even, dp, zero), jnp.where(even, zero, dp)], axis=0
            )
            inside.append(dot(jnp.concatenate(mixes, axis=1), stacked))
            which = (pick == 2 * j + half).astype(F32).astype(BF16)
            which_t = (pickt == 2 * j + halft).astype(F32).astype(BF16)
            by_source = by_source + dot(jnp.concatenate(flows, axis=1), which)
            by_target = by_target + dot(which_t, jnp.concatenate(flows, axis=0))
        d_scaled = d_weighted * fade + jnp.concatenate(inside, axis=1)
        db = db + three_dots(dscores_t, r)
        dc = dc_ref[rows, :] + three_dots(dscores_t, b, TN)
        d_running = by_target.T - by_source + q_ref[rows, :] - used
        d_last = jnp.sum(used, axis=0, keepdims=True) + held
        d_decay = dot_exact_left3(upper, d_running) + d_last
        d_delta = dot_exact_right(d_scaled * v, cols) - rate * d_decay
        gd_ref[rows, :] = (d_delta * sigmoid(raw)).astype(BF16)
        gp_ref[rows, 0:D] = (d_scaled * widened + skip * dy).astype(BF16)
        gp_ref[rows, D:PROJ] = jnp.concatenate([db, dc], axis=1).astype(BF16)
        grad_ref[...] = r_ref[c] + keep * grad
        return 0

    lax.fori_loop(0, NC, chunk, 0)

    def send_back(c, _):
        rows = pl.ds(pl.multiple_of(c * L, L), L)
        gs = dot(gp_ref[rows, :], wp_ref[...], NT) + dot(gd_ref[rows, :], wd_ref[...], NT)
        gs = gs.astype(BF16)
        for k in range(L // BLK):
            ret_ref[dst_ref[0, c * (L // BLK) + k]] = gs[BLK * k:BLK * k + BLK]
        return 0

    lax.fori_loop(0, NC, send_back, 0)

    gp = gp_ref[...]
    gd = gd_ref[...]
    low = low_ref[...]
    for m in range(8):
        lanes = slice(128 * m, 128 * m + 128)
        xt = x_ref[:, lanes].T
        gt = g_ref[:, lanes].T
        proj_rows = dot(xt, gp).astype(BF16)
        out_rows = dot(gt, low).astype(BF16)
        dt_rows = dot(xt, gd)
        dt_hi, dt_lo = split2(dt_rows)
        dt_rows = jnp.concatenate([dt_hi, dt_lo, jnp.zeros((128, 128 - 2 * H), BF16)], axis=1)
        for k in range(4):
            d = 4 * m + k
            y, xx, core = d >> 3, (d >> 1) & 3, d & 1
            sub = slice(32 * k, 32 * k + 32)
            p1_ref[core, xx, y] = proj_rows[sub]
            p2_ref[core, y, xx, :, 0:D] = out_rows[sub]
            p2_ref[core, y, xx, :, D:PROJ] = dt_rows[sub]


def backward(src, dst, leaving, x, g, v, bc, raw, run, runt, dy, low, q, dc, s, r,
             w_proj, w_dt, rate, skip):
    part = jax.ShapeDtypeStruct((2, 4, 4, 32, PROJ), BF16)
    return pl.pallas_call(
        backward_kernel,
        out_shape=[
            jax.ShapeDtypeStruct((NSEQ, BLK, D), BF16),
            jax.ShapeDtypeStruct((1, NSEQ), jnp.int32),
            part,
            part,
        ],
        in_specs=[SM, SM] + [VM] * 18,
        out_specs=[VM, SM, VM, VM],
        scratch_shapes=[
            pltpu.VMEM((N, D), F32), pltpu.VMEM((T, PROJ), BF16), pltpu.VMEM((T, H), BF16)
        ],
        compiler_params=pltpu.CompilerParams(vmem_limit_bytes=VMEM_LIMIT),
        name="backward",
    )(src, dst, leaving, x, g, v, bc, raw, run, runt, dy, low, q, dc, s, r,
      w_proj, w_dt, rate, skip)


def places():
    z = lax.axis_index("dp")
    me = lax.axis_index("seq")
    y = me // 8
    x = lax.rem(me // 2, 4)
    core = lax.rem(me, 2)
    return z, y, x, core


def narrow(total):
    return total.astype(BF16)


def narrow_pairs(total):
    tail = total[:, D:PROJ]
    high = tail.astype(BF16).astype(F32)
    rest = (tail - high)[:, 0:H]
    width = tail.shape[1]
    moved = jnp.concatenate(
        [jnp.zeros_like(rest), rest, jnp.zeros((rest.shape[0], width - 2 * H), F32)], axis=1
    )
    lane = iota(tail.shape, 1)
    tail = jnp.where(lane < H, high, tail + moved)
    return jnp.concatenate([total[:, 0:D], tail], axis=1).astype(BF16)


def reduce_kernel(p1_ref, p2_ref, gp_ref, gd_ref, go_ref,
                  ra1, ra2, t1, t2, rb1, rb2, h1, h2, rc1, rc2, zs, zr, zo,
                  sa, qa, sb, qb, sc, qc, sz, qz, so, qo):
    z, y, x, core = places()
    seq = 8 * y + 2 * x + core
    partner = (z, seq + 1 - 2 * core)

    def at_x(k):
        return (z, 8 * y + 2 * lax.rem(x + k, 4) + core)

    def at_y(k):
        return (z, 8 * lax.rem(y + k, 4) + 2 * x + core)

    def at_z(k):
        return (lax.rem(z + k, NDP), seq)

    barrier = pltpu.get_barrier_semaphore()
    pl.semaphore_signal(barrier, inc=1, device_id=partner, device_id_type=MESH)
    for k in (1, 2, 3):
        pl.semaphore_signal(barrier, inc=1, device_id=at_x(k), device_id_type=MESH)
        pl.semaphore_signal(barrier, inc=1, device_id=at_y(k), device_id_type=MESH)
    for k in range(1, NDP):
        pl.semaphore_signal(barrier, inc=1, device_id=at_z(k), device_id_type=MESH)
    pl.semaphore_wait(barrier, 14)

    a1 = to_peer(p1_ref.at[1 - core], ra1, sa.at[0], qa.at[0], partner)
    a2 = to_peer(p2_ref.at[1 - core], ra2, sa.at[1], qa.at[1], partner)
    a1.start()
    a2.start()

    def hop(src, dst, send, recv, first, here, place):
        copies = []
        for k in (1, 2, 3):
            to = lax.rem(here + k, 4)
            frm = lax.rem(here - k + 4, 4)
            copies.append((
                to_peer(src.at[to], dst.at[here], send.at[first + to], recv.at[first + here],
                        place(k)),
                to_peer(src.at[to], dst.at[frm], send.at[first + to], recv.at[first + frm],
                        place(k)),
            ))
        return copies

    b1 = hop(t1, rb1, sb, qb, 0, x, at_x)
    b2 = hop(t2, rb2, sb, qb, 4, y, at_y)
    c1 = hop(h1, rc1, sc, qc, 0, y, at_y)
    c2 = hop(h2, rc2, sc, qc, 4, x, at_x)

    def add_pair(p_ref, ra, t, form):
        def body(i, _):
            a, b = i // 4, lax.rem(i, 4)
            t[a, b] = form(p_ref[core, a, b].astype(F32) + ra[a, b].astype(F32))
            return 0

        lax.fori_loop(0, 16, body, 0)

    a1.wait()
    add_pair(p1_ref, ra1, t1, narrow)
    for go, _ in b1:
        go.start()
    a2.wait()
    add_pair(p2_ref, ra2, t2, narrow_pairs)
    for go, _ in b2:
        go.start()

    def first_sum(t, rb, h, here, copies, form):
        for _, got in copies:
            got.wait_send()
            got.wait_recv()

        def body(b, _):
            total = t[here, b].astype(F32)
            for k in (1, 2, 3):
                total = total + rb[lax.rem(here + k, 4), b].astype(F32)
            h[b] = form(total)
            return 0

        lax.fori_loop(0, 4, body, 0)

    first_sum(t1, rb1, h1, x, b1, narrow)
    for go, _ in c1:
        go.start()
    first_sum(t2, rb2, h2, y, b2, narrow_pairs)
    for go, _ in c2:
        go.start()

    def second_sum(h, rc, here, copies):
        for _, got in copies:
            got.wait_send()
            got.wait_recv()
        total = h[here].astype(F32)
        for k in (1, 2, 3):
            total = total + rc[lax.rem(here + k, 4)].astype(F32)
        return total

    s1 = second_sum(h1, rc1, y, c1)
    for i in range(4):
        zs[i] = s1[8 * i:8 * i + 8]
    s2 = second_sum(h2, rc2, x, c2)
    for i in range(4):
        zs[4 + i] = s2[8 * i:8 * i + 8]

    def z_out(k, _):
        to = lax.rem(z + k, NDP)
        to_peer(zs.at[to], zr.at[z], sz.at[to], qz.at[z], at_z(k)).start()
        return 0

    lax.fori_loop(1, NDP, z_out, 0)

    def z_done(k, total):
        to = lax.rem(z + k, NDP)
        frm = lax.rem(z - k + NDP, NDP)
        copy = to_peer(zs.at[to], zr.at[frm], sz.at[to], qz.at[frm], at_z(k))
        copy.wait_send()
        copy.wait_recv()
        return total + zr[frm]

    total = lax.fori_loop(1, NDP, z_done, zs[z])
    zo[z] = total * ((NDP * NSEQ * T) ** (-0.5))

    def o_out(k, _):
        to_peer(zo.at[z], zo.at[z], so.at[k], qo.at[z], at_z(k)).start()
        return 0

    lax.fori_loop(1, NDP, o_out, 0)

    def o_done(k, _):
        frm = lax.rem(z - k + NDP, NDP)
        copy = to_peer(zo.at[z], zo.at[frm], so.at[k], qo.at[frm], at_z(k))
        copy.wait_send()
        copy.wait_recv()
        return 0

    lax.fori_loop(1, NDP, o_done, 0)
    for i in range(4):
        gp_ref[8 * i:8 * i + 8, :] = zo[i]
        gd_ref[8 * i:8 * i + 8, :] = zo[4 + i, :, D:PROJ]
        go_ref[8 * i:8 * i + 8, :] = zo[4 + i, :, 0:D]


def reduce_all(p1, p2):
    part = pltpu.VMEM((4, 4, 32, PROJ), BF16)
    line = pltpu.VMEM((4, 32, PROJ), BF16)
    zed = pltpu.VMEM((NDP, 8, PROJ), F32)
    dma = pltpu.SemaphoreType.DMA
    return pl.pallas_call(
        reduce_kernel,
        out_shape=[
            jax.ShapeDtypeStruct((32, PROJ), F32),
            jax.ShapeDtypeStruct((32, 128), F32),
            jax.ShapeDtypeStruct((32, D), F32),
        ],
        in_specs=[VM] * 2,
        out_specs=[VM] * 3,
        scratch_shapes=[part] * 6 + [line] * 4 + [zed] * 3
        + [dma((2,)), dma((2,)), dma((8,)), dma((8,)), dma((8,)), dma((8,)),
           dma((8,)), dma((8,)), dma((8,)), dma((8,))],
        compiler_params=pltpu.CompilerParams(
            collective_id=4, has_side_effects=True, vmem_limit_bytes=VMEM_LIMIT
        ),
        name="reduce_all",
    )(p1, p2)


def local(tokens, grad_out, src_order, dst_order, w_proj, w_dt, w_out,
          dt_bias, decay_rate, d_skip, norm_gain):
    blocks = (NSEQ, BLK, D)
    bias = dt_bias.reshape(1, H)
    rate = decay_rate.reshape(1, H)
    skip = d_skip.reshape(1, H)
    gain = norm_gain.reshape(1, D)
    x, g = enter(tokens.reshape(blocks), grad_out.reshape(blocks), src_order, dst_order)
    x = x.reshape(T, D)
    g = g.reshape(T, D)
    v, bc, raw, run, runt, u, pay = project(x, w_proj, w_dt, bias, rate)
    entering = relay(pay, False)
    dy, low, q, dc, s, r, pay_back = forward(
        entering, v, bc, raw, run, runt, u, g, w_out, skip, gain
    )
    leaving = relay(pay_back, True)
    returning, inverse, p1, p2 = backward(
        src_order, dst_order, leaving, x, g, v, bc, raw, run, runt, dy, low, q, dc, s, r,
        w_proj, w_dt, rate, skip
    )
    grad_tokens = leave(inverse, returning)
    gp, gd, go = reduce_all(p1, p2)
    return grad_tokens.reshape(1, T, D), gp, gd[:, 0:H] + gd[:, H:2 * H], go.T


def solution(mesh):
    in_specs = (
        P("dp", "seq", None), P("dp", "seq", None), P("seq", None), P("seq", None),
        P(), P(), P(), P(), P(), P(), P(),
    )
    out_specs = (P("dp", "seq", None), P("seq", None), P("seq", None), P(None, "seq"))
    return jax.shard_map(local, mesh=mesh, in_specs=in_specs, out_specs=out_specs, check_vma=False)
```

```python
import functools

import jax
import jax.numpy as jnp
from jax import lax
from jax.experimental import pallas as pl
from jax.experimental.pallas import tpu as pltpu
from jax.sharding import PartitionSpec as P

H = 16
P_SIZE = 64
N = 64
D = 1024
PROJ = 1152
BLK = 16
NSEQ = 32
NDP = 8
T = 512
L = 128
NC = T // L
EPSILON = 1e-05
F32 = jnp.float32
BF16 = jnp.bfloat16
MESH = pl.DeviceIdType.MESH
VMEM_LIMIT = 62 * 1024 * 1024
HALF = 640

VM = pl.BlockSpec(memory_space=pltpu.VMEM)
SM = pl.BlockSpec(memory_space=pltpu.SMEM)

NN = (((1,), (0,)), ((), ()))
NT = (((1,), (1,)), ((), ()))
TN = (((0,), (0,)), ((), ()))


def dot(a, b, dims=NN):
    return lax.dot_general(a, b, dims, preferred_element_type=F32)


def split2(a):
    hi = a.astype(BF16)
    return hi, (a - hi.astype(F32)).astype(BF16)


def split3(a):
    hi, mid = split2(a)
    low = a - hi.astype(F32) - mid.astype(F32)
    return hi, mid, low.astype(BF16)


def dot_exact_right(a, b, dims=NN):
    hi, lo = split2(a)
    return dot(hi, b, dims) + dot(lo, b, dims)


def dot_exact_left3(a, b):
    hi, mid, low = split3(b)
    return (dot(a, low) + dot(a, mid)) + dot(a, hi)


def wide_dot(a, b, dims=NN):
    ka, kb = dims[0][0][0], dims[0][1][0]
    ah, al = split2(a)
    bh, bl = split2(b)
    return dot(
        jnp.concatenate([ah, al, ah], axis=ka), jnp.concatenate([bh, bh, bl], axis=kb), dims
    )


def three_dots(a, b, dims=NN):
    ah, al = split2(a)
    bh, bl = split2(b)
    return (dot(al, bh, dims) + dot(ah, bl, dims)) + dot(ah, bh, dims)


def iota(shape, dim):
    return lax.broadcasted_iota(jnp.int32, shape, dim)


def head_rows():
    return ((iota((H, D), 1) >> 6) == iota((H, D), 0)).astype(F32).astype(BF16)


def head_columns():
    return ((iota((D, H), 0) >> 6) == iota((D, H), 1)).astype(F32).astype(BF16)


def lower_ones():
    return (iota((L, L), 0) >= iota((L, L), 1)).astype(F32).astype(BF16)


def upper_ones():
    return (iota((L, L), 0) <= iota((L, L), 1)).astype(F32).astype(BF16)


def softplus(v):
    return jnp.maximum(v, 0.0) + jnp.log1p(jnp.exp(-jnp.abs(v)))


def sigmoid(v):
    e = jnp.exp(-jnp.abs(v))
    return jnp.where(v >= 0, 1.0, e) / (1.0 + e)


def pack_payload(pay_ref, state, keep):
    for rg in range(8):
        for lg in range(4):
            lanes = slice(256 * lg, 256 * lg + 256)
            pay_ref[rg * 4 + lg, 0:8, :] = state[8 * rg:8 * rg + 8, lanes]
            pay_ref[rg * 4 + lg, 8:16, :] = jnp.broadcast_to(keep[:, lanes], (8, 256))


def unpack_state(ref, state_ref):
    for rg in range(8):
        for lg in range(4):
            state_ref[8 * rg:8 * rg + 8, 256 * lg:256 * lg + 256] = ref[rg * 4 + lg]


def to_peer(src, dst, send_sem, recv_sem, peer):
    return pltpu.make_async_remote_copy(
        src_ref=src, dst_ref=dst, send_sem=send_sem, recv_sem=recv_sem,
        device_id=peer, device_id_type=MESH,
    )


def places():
    z = lax.axis_index("dp")
    me = lax.axis_index("seq")
    return z, me // 8, lax.rem(me // 2, 4), lax.rem(me, 2)


def greet():
    z = lax.axis_index("dp")
    me = lax.axis_index("seq")
    barrier = pltpu.get_barrier_semaphore()

    def hello(k, _):
        pl.semaphore_signal(
            barrier, inc=1, device_id=(z, lax.rem(me + k, NSEQ)), device_id_type=MESH
        )
        return 0

    def hello_z(k, _):
        pl.semaphore_signal(
            barrier, inc=1, device_id=(lax.rem(z + k, NDP), me), device_id_type=MESH
        )
        return 0

    lax.fori_loop(1, NSEQ, hello, 0)
    lax.fori_loop(1, NDP, hello_z, 0)


def greeted():
    pl.semaphore_wait(pltpu.get_barrier_semaphore(), NSEQ - 1 + NDP - 1)


class Exchange:
    def __init__(self, send, recv, sems):
        self.send, self.recv = send, recv
        self.ss, self.rs = sems.at[0], sems.at[1]

    def start(self):
        z = lax.axis_index("dp")
        me = lax.axis_index("seq")

        def go(k, _):
            to = lax.rem(me + k, NSEQ)
            to_peer(self.send.at[to], self.recv.at[me], self.ss, self.rs, (z, to)).start()
            return 0

        lax.fori_loop(1, NSEQ, go, 0)

    def wait(self):
        z = lax.axis_index("dp")
        me = lax.axis_index("seq")
        most = pl.ds(0, NSEQ - 1)
        copy = to_peer(self.send.at[most], self.recv.at[most], self.ss, self.rs,
                       (z, lax.rem(me + 1, NSEQ)))
        copy.wait_send()
        copy.wait_recv()


def narrow(total):
    return total.astype(BF16)


def narrow_pairs(total):
    start = total.shape[1] - 128
    tail = total[:, start:]
    high = tail.astype(BF16).astype(F32)
    rest = (tail - high)[:, 0:H]
    moved = jnp.concatenate(
        [jnp.zeros_like(rest), rest, jnp.zeros((rest.shape[0], 128 - 2 * H), F32)], axis=1
    )
    lane = iota(tail.shape, 1)
    tail = jnp.where(lane < H, high, tail + moved)
    return jnp.concatenate([total[:, 0:start], tail], axis=1).astype(BF16)


class PlaneSum:
    def __init__(self, part, ra, t, rb, h, rc, sems, x_first, form):
        self.part, self.ra, self.t, self.rb, self.h, self.rc = part, ra, t, rb, h, rc
        self.sems, self.form = sems, form
        z, y, x, core = places()
        self.core = core
        at_x = lambda k: (z, 8 * y + 2 * lax.rem(x + k, 4) + core)
        at_y = lambda k: (z, 8 * lax.rem(y + k, 4) + 2 * x + core)
        self.first = (x, at_x) if x_first else (y, at_y)
        self.second = (y, at_y) if x_first else (x, at_x)
        partner = (z, 8 * y + 2 * x + 1 - core)
        self.pair = to_peer(part.at[1 - core], ra, sems.at[0], sems.at[1], partner)

    def hop(self, src, dst, where, sem):
        here, place = where
        for k in (1, 2, 3):
            to_peer(src.at[lax.rem(here + k, 4)], dst.at[here],
                    self.sems.at[sem], self.sems.at[sem + 1], place(k)).start()

    def hopped(self, src, dst, where, sem):
        here, place = where
        most = pl.ds(0, 3)
        copy = to_peer(src.at[most], dst.at[most], self.sems.at[sem], self.sems.at[sem + 1],
                       place(1))
        copy.wait_send()
        copy.wait_recv()

    def start_pair(self):
        self.pair.start()

    def start_first(self):
        self.pair.wait()

        def body(i, _):
            a, b = i // 4, lax.rem(i, 4)
            self.t[a, b] = self.form(
                self.part[self.core, a, b].astype(F32) + self.ra[a, b].astype(F32)
            )
            return 0

        lax.fori_loop(0, 16, body, 0)
        self.hop(self.t, self.rb, self.first, 2)

    def start_second(self):
        self.hopped(self.t, self.rb, self.first, 2)
        here = self.first[0]

        def body(b, _):
            total = self.t[here, b].astype(F32)
            for k in (1, 2, 3):
                total = total + self.rb[lax.rem(here + k, 4), b].astype(F32)
            self.h[b] = self.form(total)
            return 0

        lax.fori_loop(0, 4, body, 0)
        self.hop(self.h, self.rc, self.second, 4)

    def finish(self):
        self.hopped(self.h, self.rc, self.second, 4)
        here = self.second[0]
        total = self.h[here].astype(F32)
        for k in (1, 2, 3):
            total = total + self.rc[lax.rem(here + k, 4)].astype(F32)
        return total


class DepthSum:
    def __init__(self, zs, zr, zo, sems):
        self.zs, self.zr, self.zo, self.sems = zs, zr, zo, sems
        self.z = lax.axis_index("dp")
        self.me = lax.axis_index("seq")

    def out(self, source, target, sem):
        def go(k, _):
            to = lax.rem(self.z + k, NDP)
            to_peer(source(to), target, self.sems.at[sem], self.sems.at[sem + 1],
                    (to, self.me)).start()
            return 0

        lax.fori_loop(1, NDP, go, 0)

    def done(self, src, dst, sem):
        most = pl.ds(0, NDP - 1)
        copy = to_peer(src.at[most], dst.at[most], self.sems.at[sem], self.sems.at[sem + 1],
                       (lax.rem(self.z + 1, NDP), self.me))
        copy.wait_send()
        copy.wait_recv()

    def start(self):
        self.out(lambda to: self.zs.at[to], self.zr.at[self.z], 0)

    def spread(self):
        self.done(self.zs, self.zr, 0)

        def add(k, total):
            return total + self.zr[lax.rem(self.z + k, NDP)]

        total = lax.fori_loop(1, NDP, add, self.zs[self.z])
        self.zo[self.z] = total * ((NDP * NSEQ * T) ** (-0.5))
        self.out(lambda to: self.zo.at[self.z], self.zo.at[self.z], 2)

    def finish(self):
        self.done(self.zo, self.zo, 2)


def relay_prefix(recv, mid, reverse):
    def step(i, state):
        j = NSEQ - 1 - i if reverse else i
        mid[j] = state
        return recv[j, 8:16] * state + recv[j, 0:8]

    lax.fori_loop(0, NSEQ, step, jnp.zeros((8, 256), F32))


def chunk_rows(c):
    return pl.ds(pl.multiple_of(c * L, L), L)


def keep_row(last, heads):
    return dot_exact_right(jnp.broadcast_to(jnp.exp(last), (8, H)), heads)[0:1]


def keep_row3(total, heads):
    hi, mid, low = split3(jnp.broadcast_to(jnp.exp(total), (8, H)))
    return ((dot(low, heads) + dot(mid, heads)) + dot(hi, heads))[0:1]


def whole_kernel(
    src_ref, dst_ref, isrc_ref, idst_ref, tok_hbm, grad_hbm, wp_hbm, wd_hbm, wo_hbm,
    bias_ref, rate_ref, skip_ref, gain_ref,
    out_ref, gp_out, gd_out, go_out,
    tok, grd, wp, wd, wo, send_t, send_g, recv_t, recv_g, x_ref, g_ref,
    v_ref, bc_ref, raw_ref, run_ref, runt_ref, u_ref, sc_ref, wid_ref, fade_ref,
    pay1, got1, mid1, ent1, pay2, got2, mid2, ent2,
    yin_ref, gn_ref, dy_ref, low_ref, q_ref, dc_ref, db_ref, s_ref, r_ref,
    state_ref, gp_ref, gd_ref, ret, back,
    pa, ra_a, ta, rb_a, ha, rc_a, pb, ra_b, tb, rb_b, hb, rc_b, pw, ra_w, tw, rb_w, hw, rc_w,
    zs1, zr1, zo1, zs2, zr2, zo2,
    load_sems, st_sems, sg_sems, r1_sems, r2_sems, r3_sems, r4_sems, lv_sems,
    a_sems, b_sems, w_sems, z1_sems, z2_sems,
):
    me = lax.axis_index("seq")
    loads = [
        pltpu.make_async_copy(a, b, load_sems.at[i])
        for i, (a, b) in enumerate(
            [(tok_hbm, tok), (grad_hbm, grd), (wp_hbm, wp), (wd_hbm, wd), (wo_hbm, wo)]
        )
    ]
    for load in loads:
        load.start()
    greet()
    tokens_in = Exchange(send_t, recv_t, st_sems)
    grads_in = Exchange(send_g, recv_g, sg_sems)
    loads[0].wait()

    def load_t(d, _):
        send_t[d] = tok[src_ref[0, d]]
        return 0

    def load_g(d, _):
        send_g[d] = grd[src_ref[0, d]]
        return 0

    lax.fori_loop(0, NSEQ, load_t, 0)
    greeted()
    tokens_in.start()
    loads[1].wait()
    lax.fori_loop(0, NSEQ, load_g, 0)
    grads_in.start()
    recv_t[me] = send_t[me]
    recv_g[me] = send_g[me]

    heads = head_rows()
    cols = head_columns()
    lower = lower_ones()
    upper = upper_ones()
    even = iota((1, 128), 1) < 64
    bias = bias_ref[...]
    rate = rate_ref[...]
    gain = gain_ref[...]
    skip = dot_exact_right(jnp.broadcast_to(skip_ref[...], (8, H)), heads)[0:1]
    loads[2].wait()
    loads[3].wait()
    loads[4].wait()
    tokens_in.wait()

    def settle_t(j, _):
        x_ref[pl.ds(pl.multiple_of(j * BLK, BLK), BLK), :] = recv_t[dst_ref[0, j]]
        return 0

    lax.fori_loop(0, NSEQ, settle_t, 0)

    def project(c, carry):
        state, total = carry
        rows = chunk_rows(c)
        x = x_ref[rows, :]
        v = dot(x, wp[:, 0:D])
        v_ref[rows, :] = v
        bc = dot(x, wp[:, D:PROJ])
        bc_ref[rows, :] = bc
        raw = dot(x, wd[...], NT) + bias
        raw_ref[rows, :] = raw
        delta = softplus(raw)
        running = dot_exact_left3(lower, -rate * delta)
        run_ref[rows, :] = running
        runt_ref[c] = running.T
        last = running[L - 1:L, :]
        widened = dot_exact_right(delta, heads)
        wid_ref[rows, :] = widened
        scaled = v * widened
        sc_ref[rows, :] = scaled
        fade = dot_exact_right(jnp.exp(last - running), heads)
        fade_ref[rows, :] = fade
        added = wide_dot(bc[:, 0:N], scaled * fade, TN)
        u_ref[c] = added
        return keep_row(last, heads) * state + added, total + last

    state, total = lax.fori_loop(
        0, NC, project, (jnp.zeros((N, D), F32), jnp.zeros((1, H), F32))
    )
    keep_all = keep_row3(total, heads)
    pack_payload(pay1, state, keep_all)
    ahead = Exchange(pay1, got1, r1_sems)
    ahead.start()
    got1[me] = pay1[me]

    below = iota((L, L), 0) >= iota((L, L), 1)

    def inside_forward(c, _):
        rows = chunk_rows(c)
        bc = bc_ref[rows, :]
        running = run_ref[rows, :]
        runt = runt_ref[c]
        scores = wide_dot(bc[:, N:2 * N], bc[:, 0:N], NT)
        scaled = sc_ref[rows, :].astype(BF16)
        for j in range(H // 2):
            mixes = []
            for h in (2 * j, 2 * j + 1):
                spread = running[:, h:h + 1] - runt[h:h + 1, :]
                decay = jnp.exp(jnp.where(below, spread, -jnp.inf))
                mixes.append((decay * scores).astype(BF16))
            pair = scaled[:, 128 * j:128 * j + 128]
            zero = jnp.zeros_like(pair)
            stacked = jnp.concatenate(
                [jnp.where(even, pair, zero), jnp.where(even, zero, pair)], axis=0
            )
            yin_ref[rows, 128 * j:128 * j + 128] = dot(jnp.concatenate(mixes, axis=1), stacked)
        return 0

    lax.fori_loop(0, 2, inside_forward, 0)
    ahead.wait()
    relay_prefix(got1, mid1, False)
    ahead_back = Exchange(mid1, ent1, r2_sems)
    ahead_back.start()
    ent1[me] = mid1[me]
    lax.fori_loop(2, NC, inside_forward, 0)
    grads_in.wait()

    def settle_g(j, _):
        g_ref[pl.ds(pl.multiple_of(j * BLK, BLK), BLK), :] = recv_g[dst_ref[0, j]]
        return 0

    lax.fori_loop(0, NSEQ, settle_g, 0)

    def project_grads(c, _):
        rows = chunk_rows(c)
        gn_ref[rows, :] = dot(g_ref[rows, :], wo[...], NT) * gain
        return 0

    lax.fori_loop(0, NC, project_grads, 0)
    ahead_back.wait()
    unpack_state(ent1, state_ref)

    def forward(c, carry):
        out_grad, before = carry
        rows = chunk_rows(c)
        r = bc_ref[rows, N:2 * N]
        running = run_ref[rows, :]
        last = running[L - 1:L, :]
        state = state_ref[...]
        s_ref[c] = state
        grown = dot_exact_right(jnp.exp(running), heads)
        carried = wide_dot(r, state) * grown
        summed = yin_ref[rows, :] + carried + skip * v_ref[rows, :]
        square = dot_exact_right(summed * summed, cols) * (1.0 / P_SIZE)
        scale = dot_exact_right(lax.rsqrt(square + EPSILON), heads)
        unit = summed * scale
        low_ref[rows, :] = (unit * gain).astype(BF16)
        grad_unit = gn_ref[rows, :]
        along = dot_exact_right(grad_unit * unit, cols) * (1.0 / P_SIZE)
        dy = scale * (grad_unit - unit * dot_exact_right(along, heads))
        dy_ref[rows, :] = dy
        q_ref[rows, :] = dot_exact_right(dy * carried, cols)
        back_in = dy * grown
        dc_ref[rows, :] = three_dots(back_in, state, NT)
        reach = wide_dot(r, back_in, TN)
        r_ref[c] = reach
        keep = keep_row(last, heads)
        state_ref[...] = keep * state + u_ref[c]
        return out_grad + before * reach, before * keep

    out_grad, _ = lax.fori_loop(
        0, NC, forward, (jnp.zeros((N, D), F32), jnp.ones((1, D), F32))
    )
    pack_payload(pay2, out_grad, keep_all)
    astern = Exchange(pay2, got2, r3_sems)
    astern.start()
    got2[me] = pay2[me]

    sum_a = PlaneSum(pa, ra_a, ta, rb_a, ha, rc_a, a_sems, True, narrow)
    sum_b = PlaneSum(pb, ra_b, tb, rb_b, hb, rc_b, b_sems, False, narrow_pairs)
    sum_w = PlaneSum(pw, ra_w, tw, rb_w, hw, rc_w, w_sems, True, narrow)
    deep1 = DepthSum(zs1, zr1, zo1, z1_sems)
    deep2 = DepthSum(zs2, zr2, zo2, z2_sems)

    def spots(m):
        for k in range(4):
            d = 4 * m + k
            yield d >> 3, (d >> 1) & 3, d & 1, slice(32 * k, 32 * k + 32)

    low = low_ref[...]
    for m in range(8):
        gt = g_ref[:, 128 * m:128 * m + 128].T
        out_rows = dot(gt, low).astype(BF16)
        for y, x, core, sub in spots(m):
            pw[core, x, y] = out_rows[sub]
    sum_w.start_pair()
    astern.wait()
    relay_prefix(got2, mid2, True)
    astern_back = Exchange(mid2, ent2, r4_sems)
    astern_back.start()
    ent2[me] = mid2[me]
    sum_w.start_first()

    after = iota((L, L), 1) >= iota((L, L), 0)
    half = iota((2 * L, H), 0) >> 7
    pick = iota((2 * L, H), 1)
    halft = iota((H, 2 * L), 1) >> 7
    pickt = iota((H, 2 * L), 0)

    def inside_backward(c, _):
        rows = chunk_rows(c)
        bc = bc_ref[rows, :]
        b, r = bc[:, 0:N], bc[:, N:2 * N]
        running = run_ref[rows, :]
        runt = runt_ref[c]
        dy_low = dy_ref[rows, :].astype(BF16)
        scaled = sc_ref[rows, :].astype(BF16)
        scores_t = wide_dot(b, r, NT)
        dscores_t = jnp.zeros((L, L), F32)
        by_source = jnp.zeros((L, H), F32)
        by_target = jnp.zeros((H, L), F32)
        for j in range(H // 2):
            pair = slice(128 * j, 128 * j + 128)
            sp = scaled[:, pair]
            dp = dy_low[:, pair]
            zero = jnp.zeros_like(sp)
            mixes, flows = [], []
            for e in (0, 1):
                h = 2 * j + e
                spread = runt[h:h + 1, :] - running[:, h:h + 1]
                decay = jnp.exp(jnp.where(after, spread, -jnp.inf))
                mixes.append((decay * scores_t).astype(BF16))
                mine = jnp.where(even, sp, zero) if e == 0 else jnp.where(even, zero, sp)
                moved = dot(mine, dp, NT) * decay
                dscores_t = dscores_t + moved
                flows.append((moved * scores_t).astype(BF16))
            stacked = jnp.concatenate(
                [jnp.where(even, dp, zero), jnp.where(even, zero, dp)], axis=0
            )
            yin_ref[rows, pair] = dot(jnp.concatenate(mixes, axis=1), stacked)
            which = (pick == 2 * j + half).astype(F32).astype(BF16)
            which_t = (pickt == 2 * j + halft).astype(F32).astype(BF16)
            by_source = by_source + dot(jnp.concatenate(flows, axis=1), which)
            by_target = by_target + dot(which_t, jnp.concatenate(flows, axis=0))
        db_ref[rows, :] = three_dots(dscores_t, r)
        dc_ref[rows, :] = dc_ref[rows, :] + three_dots(dscores_t, b, TN)
        q_ref[rows, :] = q_ref[rows, :] + (by_target.T - by_source)
        return 0

    lax.fori_loop(0, 2, inside_backward, 0)
    sum_w.start_second()
    lax.fori_loop(2, NC, inside_backward, 0)
    sum_rows = sum_w.finish()
    for i in range(4):
        for k in range(2):
            zs2[4 * k + i] = sum_rows[8 * i:8 * i + 8, 512 * k:512 * k + 512]
    deep2.start()
    astern_back.wait()
    unpack_state(ent2, state_ref)

    def backward(i, _):
        c = NC - 1 - i
        rows = chunk_rows(c)
        bc = bc_ref[rows, :]
        b = bc[:, 0:N]
        running = run_ref[rows, :]
        last = running[L - 1:L, :]
        grad = state_ref[...]
        fade = fade_ref[rows, :]
        weighted = sc_ref[rows, :] * fade
        d_weighted = wide_dot(b, grad)
        used = dot_exact_right(d_weighted * weighted, cols)
        db = db_ref[rows, :] + three_dots(weighted, grad, NT)
        keep = keep_row(last, heads)
        held = jnp.sum(keep * grad * s_ref[c], axis=0, keepdims=True)
        held = dot_exact_right(jnp.broadcast_to(held, (8, D)), cols)[0:1]
        d_scaled = d_weighted * fade + yin_ref[rows, :]
        d_running = q_ref[rows, :] - used
        d_last = jnp.sum(used, axis=0, keepdims=True) + held
        d_decay = dot_exact_left3(upper, d_running) + d_last
        d_delta = dot_exact_right(d_scaled * v_ref[rows, :], cols) - rate * d_decay
        gd = (d_delta * sigmoid(raw_ref[rows, :])).astype(BF16)
        gd_ref[rows, :] = gd
        gp_ref[rows, 0:D] = (d_scaled * wid_ref[rows, :] + skip * dy_ref[rows, :]).astype(BF16)
        gp_ref[rows, D:PROJ] = jnp.concatenate([db, dc_ref[rows, :]], axis=1).astype(BF16)
        state_ref[...] = r_ref[c] + keep * grad
        gs = dot(gp_ref[rows, :], wp[...], NT) + dot(gd, wd[...])
        tok[pl.ds(c * (L // BLK), L // BLK)] = gs.astype(BF16).reshape(L // BLK, BLK, D)
        return 0

    lax.fori_loop(0, NC, backward, 0)

    def send_back(d, _):
        ret[d] = tok[idst_ref[0, d]]
        return 0

    lax.fori_loop(0, NSEQ, send_back, 0)
    grads_back = Exchange(ret, back, lv_sems)
    grads_back.start()
    back[me] = ret[me]
    deep2.spread()

    gp = gp_ref[...]
    gd = gd_ref[...]
    for m in range(8):
        xt = x_ref[:, 128 * m:128 * m + 128].T
        rows_p = dot(xt, gp)
        rows_d = dot(xt, gd)
        dt_hi, dt_lo = split2(rows_d)
        rows_p = rows_p.astype(BF16)
        rows_d = jnp.concatenate([dt_hi, dt_lo, jnp.zeros((128, 128 - 2 * H), BF16)], axis=1)
        for y, x, core, sub in spots(m):
            pa[core, x, y] = rows_p[sub, 0:HALF]
            pb[core, y, x, :, 0:PROJ - HALF] = rows_p[sub, HALF:PROJ]
            pb[core, y, x, :, PROJ - HALF:HALF] = rows_d[sub]
    sum_a.start_pair()
    sum_b.start_pair()
    sum_a.start_first()
    sum_b.start_first()
    sum_a.start_second()
    sum_b.start_second()
    for k, plane in enumerate((sum_a, sum_b)):
        sum_rows = plane.finish()
        for i in range(4):
            zs1[4 * k + i] = sum_rows[8 * i:8 * i + 8]
    deep1.start()
    grads_back.wait()

    def settle_back(j, _):
        out_ref[j] = back[isrc_ref[0, j]]
        return 0

    lax.fori_loop(0, NSEQ, settle_back, 0)
    deep2.finish()
    for i in range(4):
        for k in range(2):
            go_out[8 * i:8 * i + 8, 512 * k:512 * k + 512] = zo2[4 * k + i]
    deep1.spread()
    deep1.finish()
    for i in range(4):
        rows = slice(8 * i, 8 * i + 8)
        gp_out[rows, 0:HALF] = zo1[i]
        gp_out[rows, HALF:PROJ] = zo1[4 + i, :, 0:PROJ - HALF]
        gd_out[rows, :] = zo1[4 + i, :, PROJ - HALF:HALF]


def local(tokens, grad_out, src_order, dst_order, w_proj, w_dt, w_out,
          dt_bias, decay_rate, d_skip, norm_gain):
    blocks = (NSEQ, BLK, D)
    vm = pltpu.VMEM
    dma = pltpu.SemaphoreType.DMA
    block = vm(blocks, BF16)
    full = vm((T, D), F32)
    low = vm((T, D), BF16)
    states = vm((NC, N, D), F32)
    pay, piece = vm((NSEQ, 16, 256), F32), vm((NSEQ, 8, 256), F32)

    def plane(width):
        line = vm((4, 32, width), BF16)
        square = vm((4, 4, 32, width), BF16)
        return [vm((2, 4, 4, 32, width), BF16), square, square, square, line, line]

    scratch = (
        [block, block, vm((D, PROJ), BF16), vm((H, D), BF16), vm((D, D), BF16)]
        + [block] * 4 + [low] * 2
        + [full, vm((T, 2 * N), F32), vm((T, H), F32), vm((T, H), F32), vm((NC, H, L), F32)]
        + [states] + [full] * 3
        + [pay, pay, piece, piece] * 2
        + [full, full, full, low, vm((T, H), F32), vm((T, N), F32), vm((T, N), F32)]
        + [states, states]
        + [vm((N, D), F32), vm((T, PROJ), BF16), vm((T, H), BF16), block, block]
        + plane(HALF) + plane(HALF) + plane(D)
        + [vm((NDP, 8, HALF), F32)] * 3 + [vm((NDP, 8, 512), F32)] * 3
        + [dma((5,))] + [dma((2,))] * 7 + [dma((6,))] * 3 + [dma((4,))] * 2
    )
    order = jnp.arange(NSEQ, dtype=jnp.int32)

    def inverse(perm):
        return jnp.sum(
            jnp.where(perm[0][None, :] == order[:, None], order[None, :], 0), axis=1,
            dtype=jnp.int32,
        ).reshape(1, NSEQ)

    hbm = pl.BlockSpec(memory_space=pl.ANY)
    grad_tokens, gp, gd, go = pl.pallas_call(
        whole_kernel,
        out_shape=[
            jax.ShapeDtypeStruct(blocks, BF16),
            jax.ShapeDtypeStruct((32, PROJ), F32),
            jax.ShapeDtypeStruct((32, 128), F32),
            jax.ShapeDtypeStruct((32, D), F32),
        ],
        in_specs=[SM] * 4 + [hbm] * 5 + [VM] * 4,
        out_specs=[VM] * 4,
        scratch_shapes=scratch,
        compiler_params=pltpu.CompilerParams(
            collective_id=0, has_side_effects=True, vmem_limit_bytes=VMEM_LIMIT
        ),
        name="whole",
    )(
        src_order, dst_order, inverse(src_order), inverse(dst_order),
        tokens.reshape(blocks), grad_out.reshape(blocks), w_proj, w_dt.T, w_out,
        dt_bias.reshape(1, H), decay_rate.reshape(1, H), d_skip.reshape(1, H),
        norm_gain.reshape(1, D),
    )
    return grad_tokens.reshape(1, T, D), gp, gd[:, 0:H] + gd[:, H:2 * H], go.T


def solution(mesh):
    in_specs = (
        P("dp", "seq", None), P("dp", "seq", None), P("seq", None), P("seq", None),
        P(), P(), P(), P(), P(), P(), P(),
    )
    out_specs = (P("dp", "seq", None), P("seq", None), P("seq", None), P(None, "seq"))
    return jax.shard_map(local, mesh=mesh, in_specs=in_specs, out_specs=out_specs, check_vma=False)
```

```python
import functools

import jax
import jax.numpy as jnp
from jax import lax
from jax.experimental import pallas as pl
from jax.experimental.pallas import tpu as pltpu
from jax.sharding import PartitionSpec as P

H = 16
P_SIZE = 64
N = 64
D = 1024
PROJ = 1152
BLK = 16
NSEQ = 32
NDP = 8
T = 512
L = 128
NC = T // L
EPSILON = 1e-05
F32 = jnp.float32
BF16 = jnp.bfloat16
MESH = pl.DeviceIdType.MESH
VMEM_LIMIT = 62 * 1024 * 1024
HALF = 640
SPLIT = 13
UNROLL = 2

VM = pl.BlockSpec(memory_space=pltpu.VMEM)
SM = pl.BlockSpec(memory_space=pltpu.SMEM)

NN = (((1,), (0,)), ((), ()))
NT = (((1,), (1,)), ((), ()))
TN = (((0,), (0,)), ((), ()))


def dot(a, b, dims=NN):
    return lax.dot_general(a, b, dims, preferred_element_type=F32)


def split2(a):
    hi = a.astype(BF16)
    return hi, (a - hi.astype(F32)).astype(BF16)


def split3(a):
    hi, mid = split2(a)
    low = a - hi.astype(F32) - mid.astype(F32)
    return hi, mid, low.astype(BF16)


def dot_exact_right(a, b, dims=NN):
    hi, lo = split2(a)
    return dot(hi, b, dims) + dot(lo, b, dims)


def dot_exact_left3(a, b):
    hi, mid, low = split3(b)
    return (dot(a, low) + dot(a, mid)) + dot(a, hi)


def wide_dot(a, b, dims=NN):
    ka, kb = dims[0][0][0], dims[0][1][0]
    ah, al = split2(a)
    bh, bl = split2(b)
    return dot(
        jnp.concatenate([ah, al, ah], axis=ka), jnp.concatenate([bh, bh, bl], axis=kb), dims
    )


def three_dots(a, b, dims=NN):
    ah, al = split2(a)
    bh, bl = split2(b)
    return (dot(al, bh, dims) + dot(ah, bl, dims)) + dot(ah, bh, dims)


def expand(a, heads2):
    return dot(jnp.concatenate(split2(a), axis=1), heads2)


def thrice(a, axis, second):
    hi, lo = split2(a)
    return jnp.concatenate([hi, hi, lo] if second else [hi, lo, hi], axis=axis)


def head_means(a, block):
    low = a.astype(BF16)
    return jnp.concatenate(
        [dot(low[:, 128 * j:128 * j + 128], block) for j in range(8)], axis=1
    ) * (1.0 / P_SIZE)


def iota(shape, dim):
    return lax.broadcasted_iota(jnp.int32, shape, dim)


def head_rows():
    return ((iota((H, D), 1) >> 6) == iota((H, D), 0)).astype(F32).astype(BF16)


def head_columns():
    return ((iota((D, H), 0) >> 6) == iota((D, H), 1)).astype(F32).astype(BF16)


def lower_ones():
    return (iota((L, L), 0) >= iota((L, L), 1)).astype(F32).astype(BF16)


def upper_ones():
    return (iota((L, L), 0) <= iota((L, L), 1)).astype(F32).astype(BF16)


def softplus(v):
    return jnp.maximum(v, 0.0) + jnp.log1p(jnp.exp(-jnp.abs(v)))


def sigmoid(v):
    e = jnp.exp(-jnp.abs(v))
    return jnp.where(v >= 0, 1.0, e) / (1.0 + e)


def pack_payload(pay_ref, state_ref, keep=None):
    for rg in range(8):
        for lg in range(4):
            lanes = slice(256 * lg, 256 * lg + 256)
            pay_ref[rg * 4 + lg, :, 0:256] = state_ref[8 * rg:8 * rg + 8, lanes]
            if keep is not None:
                first = keep[:, 256 * lg:256 * lg + 128]
                second = keep[:, 256 * lg + 128:256 * lg + 256]
                row = iota((8, 128), 0)
                pay_ref[rg * 4 + lg, :, 256:384] = jnp.where(row == 0, first, second)


def unpack_state(ref, state_ref):
    for rg in range(8):
        for lg in range(4):
            state_ref[8 * rg:8 * rg + 8, 256 * lg:256 * lg + 256] = ref[rg * 4 + lg]


def to_peer(src, dst, send_sem, recv_sem, peer):
    return pltpu.make_async_remote_copy(
        src_ref=src, dst_ref=dst, send_sem=send_sem, recv_sem=recv_sem,
        device_id=peer, device_id_type=MESH,
    )


def places():
    z = lax.axis_index("dp")
    me = lax.axis_index("seq")
    return z, me // 8, lax.rem(me // 2, 4), lax.rem(me, 2)


def greet():
    z = lax.axis_index("dp")
    me = lax.axis_index("seq")
    barrier = pltpu.get_barrier_semaphore()

    def hello(k, _):
        pl.semaphore_signal(
            barrier, inc=1, device_id=(z, lax.rem(me + k, NSEQ)), device_id_type=MESH
        )
        return 0

    def hello_z(k, _):
        pl.semaphore_signal(
            barrier, inc=1, device_id=(lax.rem(z + k, NDP), me), device_id_type=MESH
        )
        return 0

    for k in range(1, NSEQ):
        hello(k, 0)
    for k in range(1, NDP):
        hello_z(k, 0)


def greeted():
    pl.semaphore_wait(pltpu.get_barrier_semaphore(), NSEQ - 1 + NDP - 1)


class Exchange:
    def __init__(self, send, recv, sems):
        self.send, self.recv = send, recv
        self.ss, self.rs = sems.at[0], sems.at[1]

    def start(self, first=1, last=NSEQ):
        z = lax.axis_index("dp")
        me = lax.axis_index("seq")
        for k in range(first, last):
            to = lax.rem(me + k, NSEQ)
            to_peer(self.send.at[to], self.recv.at[me], self.ss, self.rs, (z, to)).start()

    def wait(self):
        z = lax.axis_index("dp")
        me = lax.axis_index("seq")
        most = pl.ds(0, NSEQ - 1)
        copy = to_peer(self.send.at[most], self.recv.at[most], self.ss, self.rs,
                       (z, lax.rem(me + 1, NSEQ)))
        copy.wait_send()
        copy.wait_recv()


def narrow(total):
    return total.astype(BF16)


def narrow_pairs(total):
    start = total.shape[1] - 128
    tail = total[:, start:]
    high = tail.astype(BF16).astype(F32)
    rest = (tail - high)[:, 0:H]
    moved = jnp.concatenate(
        [jnp.zeros_like(rest), rest, jnp.zeros((rest.shape[0], 128 - 2 * H), F32)], axis=1
    )
    lane = iota(tail.shape, 1)
    tail = jnp.where(lane < H, high, tail + moved)
    return jnp.concatenate([total[:, 0:start], tail], axis=1).astype(BF16)


class PlaneSum:
    def __init__(self, part, ra, t, rb, h, rc, sems, x_first, form):
        self.part, self.ra, self.t, self.rb, self.h, self.rc = part, ra, t, rb, h, rc
        self.sems, self.form = sems, form
        z, y, x, core = places()
        self.core = core
        at_x = lambda k: (z, 8 * y + 2 * lax.rem(x + k, 4) + core)
        at_y = lambda k: (z, 8 * lax.rem(y + k, 4) + 2 * x + core)
        self.first = (x, at_x) if x_first else (y, at_y)
        self.second = (y, at_y) if x_first else (x, at_x)
        partner = (z, 8 * y + 2 * x + 1 - core)
        self.pair = to_peer(part.at[1 - core], ra, sems.at[0], sems.at[1], partner)

    def hop(self, src, dst, where, sem):
        here, place = where
        for k in (1, 2, 3):
            to_peer(src.at[lax.rem(here + k, 4)], dst.at[here],
                    self.sems.at[sem], self.sems.at[sem + 1], place(k)).start()

    def hopped(self, src, dst, where, sem):
        here, place = where
        most = pl.ds(0, 3)
        copy = to_peer(src.at[most], dst.at[most], self.sems.at[sem], self.sems.at[sem + 1],
                       place(1))
        copy.wait_send()
        copy.wait_recv()

    def start_pair(self):
        self.pair.start()

    def start_first(self):
        self.pair.wait()

        def body(i, _):
            a, b = i // 4, lax.rem(i, 4)
            self.t[a, b] = self.form(
                self.part[self.core, a, b].astype(F32) + self.ra[a, b].astype(F32)
            )
            return 0

        lax.fori_loop(0, 16, body, 0)
        self.hop(self.t, self.rb, self.first, 2)

    def start_second(self):
        self.hopped(self.t, self.rb, self.first, 2)
        here = self.first[0]

        def body(b, _):
            total = self.t[here, b].astype(F32)
            for k in (1, 2, 3):
                total = total + self.rb[lax.rem(here + k, 4), b].astype(F32)
            self.h[b] = self.form(total)
            return 0

        lax.fori_loop(0, 4, body, 0)
        self.hop(self.h, self.rc, self.second, 4)

    def finish(self):
        self.hopped(self.h, self.rc, self.second, 4)
        here = self.second[0]
        total = self.h[here].astype(F32)
        for k in (1, 2, 3):
            total = total + self.rc[lax.rem(here + k, 4)].astype(F32)
        return total


class DepthSum:
    def __init__(self, zs, zr, zo, sems):
        self.zs, self.zr, self.zo, self.sems = zs, zr, zo, sems
        self.z = lax.axis_index("dp")
        self.me = lax.axis_index("seq")

    def out(self, source, target, sem):
        for k in range(1, NDP):
            to = lax.rem(self.z + k, NDP)
            to_peer(source(to), target, self.sems.at[sem], self.sems.at[sem + 1],
                    (to, self.me)).start()

    def done(self, src, dst, sem):
        most = pl.ds(0, NDP - 1)
        copy = to_peer(src.at[most], dst.at[most], self.sems.at[sem], self.sems.at[sem + 1],
                       (lax.rem(self.z + 1, NDP), self.me))
        copy.wait_send()
        copy.wait_recv()

    def start(self):
        self.out(lambda to: self.zs.at[to], self.zr.at[self.z], 0)

    def spread(self):
        self.done(self.zs, self.zr, 0)

        total = self.zs[self.z]
        for k in range(1, NDP):
            total = total + self.zr[lax.rem(self.z + k, NDP)]
        self.zo[self.z] = total * ((NDP * NSEQ * T) ** (-0.5))
        self.out(lambda to: self.zo.at[self.z], self.zo.at[self.z], 2)

    def finish(self):
        self.done(self.zo, self.zo, 2)


def relay_prefix(recv, mid, keeps, reverse):
    def step(i, state):
        j = NSEQ - 1 - i if reverse else i
        mid[j] = state
        keep = jnp.concatenate([keeps[j, 0:1, 256:384], keeps[j, 1:2, 256:384]], axis=1)
        return keep * state + recv[j, :, 0:256]

    lax.fori_loop(0, NSEQ, step, jnp.zeros((8, 256), F32), unroll=4)


def chunk_rows(c):
    return pl.ds(pl.multiple_of(c * L, L), L)


def keep_row(last, heads):
    return dot_exact_right(jnp.broadcast_to(jnp.exp(last), (8, H)), heads)[0:1]


def keep_row3(total, heads):
    hi, mid, low = split3(jnp.broadcast_to(jnp.exp(total), (8, H)))
    return ((dot(low, heads) + dot(mid, heads)) + dot(hi, heads))[0:1]


def whole_kernel(
    src_ref, dst_ref, tok_hbm, grad_hbm, wp_hbm, wd_hbm, wo_hbm,
    bias_ref, rate_ref, skip_ref, gain_ref,
    back, zo1, zo2,
    tok, grd, wp, wd, wo, wpt, wot, xt_ref, send_t, send_g, recv_t, recv_g, x_ref, g_ref,
    v_ref, bc_ref, raw_ref, run_ref, runt_ref, u_ref, sc_ref, wid_ref, fade_ref,
    pay1, got1, mid1, ent1, pay2, got2, mid2, ent2,
    yin_ref, gn_ref, dy_ref, low_ref, q_ref, dc_ref, db_ref, s_ref, r_ref,
    state_ref, keep_ref, gp_ref, gd_ref, ret, inv_ref,
    pa, ra_a, ta, rb_a, ha, rc_a, pb, ra_b, tb, rb_b, hb, rc_b,
    pv, ra_v, tv, rb_v, hv, rc_v, pw, ra_w, tw, rb_w, hw, rc_w,
    zs1, zr1, zs2, zr2,
    load_sems, st_sems, sg_sems, r1_sems, r2_sems, r3_sems, r4_sems, lv_sems,
    a_sems, b_sems, v_sems, w_sems, z1_sems, z2_sems,
):
    me = lax.axis_index("seq")
    loads = [
        pltpu.make_async_copy(a, b, load_sems.at[i])
        for i, (a, b) in enumerate(
            [(tok_hbm, tok), (grad_hbm, grd), (wp_hbm, wp), (wd_hbm, wd), (wo_hbm, wo)]
        )
    ]
    loads[0].start()
    greet()
    loads[1].start()
    tokens_in = Exchange(send_t, recv_t, st_sems)
    grads_in = Exchange(send_g, recv_g, sg_sems)
    loads[0].wait()

    def load_t(d, _):
        send_t[d] = tok[src_ref[0, d]]
        return 0

    def load_g(d, _):
        send_g[d] = grd[src_ref[0, d]]
        return 0

    def invert(s, _):
        place = 0
        for j in range(NSEQ):
            place = jnp.where(dst_ref[0, j] == s, j, place)
        inv_ref[0, s] = place
        return 0

    lax.fori_loop(0, NSEQ, load_t, 0, unroll=4)
    loads[1].wait()
    lax.fori_loop(0, NSEQ, load_g, 0, unroll=4)
    for load in loads[2:]:
        load.start()
    lax.fori_loop(0, NSEQ, invert, 0)
    greeted()
    tokens_in.start()
    grads_in.start(1, SPLIT)
    recv_t[me] = send_t[me]
    recv_g[me] = send_g[me]

    heads = head_rows()
    cols = head_columns()
    lower = lower_ones()
    upper = upper_ones()
    even = iota((1, 128), 1) < 64
    heads2 = jnp.concatenate([heads, heads], axis=0)
    block = ((iota((128, 128), 0) >> 6) == (iota((128, 128), 1) >> 6)).astype(F32).astype(BF16)
    bias = bias_ref[...]
    rate = rate_ref[...]
    gain = gain_ref[...]
    skip = dot_exact_right(jnp.broadcast_to(skip_ref[...], (8, H)), heads)[0:1]
    loads[2].wait()
    loads[3].wait()
    loads[4].wait()
    wpt[...] = wp[...].T
    wot[...] = wo[...].T
    tokens_in.wait()

    def settle_t(j, _):
        x_ref[pl.ds(pl.multiple_of(j * BLK, BLK), BLK), :] = recv_t[dst_ref[0, j]]
        return 0

    lax.fori_loop(0, NSEQ, settle_t, 0, unroll=4)

    def project(c, total):
        rows = chunk_rows(c)
        x = x_ref[rows, :]
        v = dot(x, wp[:, 0:D])
        v_ref[rows, :] = v
        bc = dot(x, wp[:, D:PROJ])
        bc_ref[rows, :] = bc
        raw = dot(x, wd[...], NT) + bias
        raw_ref[rows, :] = raw
        delta = softplus(raw)
        running = dot_exact_left3(lower, -rate * delta)
        run_ref[rows, :] = running
        runt_ref[c] = running.T
        last = running[L - 1:L, :]
        keep_ref[c] = keep_row(last, heads)
        widened = expand(delta, heads2)
        wid_ref[rows, :] = widened
        scaled = v * widened
        sc_ref[rows, :] = scaled
        fade = expand(jnp.exp(last - running), heads2)
        fade_ref[rows, :] = fade
        u_ref[c] = wide_dot(bc[:, 0:N], scaled * fade, TN)
        return total + last

    total = lax.fori_loop(0, NC, project, jnp.zeros((1, H), F32), unroll=UNROLL)
    keep_all = keep_row3(total, heads)
    state_ref[...] = u_ref[0]
    for c in range(1, NC):
        state_ref[...] = keep_ref[c] * state_ref[...] + u_ref[c]
    pack_payload(pay1, state_ref, keep_all)
    ahead = Exchange(pay1, got1, r1_sems)
    ahead.start()
    grads_in.start(SPLIT, NSEQ)
    got1[me] = pay1[me]
    xt_ref[...] = x_ref[...].T

    below = iota((L, L), 0) >= iota((L, L), 1)

    def inside_forward(c, _):
        rows = chunk_rows(c)
        bc = bc_ref[rows, :]
        running = run_ref[rows, :]
        runt = runt_ref[c]
        scores = wide_dot(bc[:, N:2 * N], bc[:, 0:N], NT)
        scaled = sc_ref[rows, :].astype(BF16)
        for j in range(H // 2):
            mixes = []
            for h in (2 * j, 2 * j + 1):
                spread = running[:, h:h + 1] - runt[h:h + 1, :]
                decay = jnp.exp(jnp.where(below, spread, -jnp.inf))
                mixes.append((decay * scores).astype(BF16))
            pair = scaled[:, 128 * j:128 * j + 128]
            zero = jnp.zeros_like(pair)
            stacked = jnp.concatenate(
                [jnp.where(even, pair, zero), jnp.where(even, zero, pair)], axis=0
            )
            yin_ref[rows, 128 * j:128 * j + 128] = dot(jnp.concatenate(mixes, axis=1), stacked)
        return 0

    lax.fori_loop(0, 3, inside_forward, 0)
    ahead.wait()
    relay_prefix(got1, mid1, got1, False)
    ahead_back = Exchange(mid1, ent1, r2_sems)
    ahead_back.start()
    ent1[me] = mid1[me]
    lax.fori_loop(3, NC, inside_forward, 0)
    grads_in.wait()

    def settle_g(j, _):
        g_ref[pl.ds(pl.multiple_of(j * BLK, BLK), BLK), :] = recv_g[dst_ref[0, j]]
        return 0

    lax.fori_loop(0, NSEQ, settle_g, 0, unroll=4)

    def project_grads(c, _):
        rows = chunk_rows(c)
        gn_ref[rows, :] = dot(g_ref[rows, :], wot[...]) * gain
        return 0

    lax.fori_loop(0, NC, project_grads, 0)
    ahead_back.wait()
    unpack_state(ent1, s_ref.at[0])
    for c in range(1, NC):
        s_ref[c] = keep_ref[c - 1] * s_ref[c - 1] + u_ref[c - 1]

    def forward(c, _):
        rows = chunk_rows(c)
        r = bc_ref[rows, N:2 * N]
        state = s_ref[c]
        grown = expand(jnp.exp(run_ref[rows, :]), heads2)
        carried = wide_dot(r, state) * grown
        summed = yin_ref[rows, :] + carried + skip * v_ref[rows, :]
        scale = lax.rsqrt(head_means(summed * summed, block) + EPSILON)
        unit = summed * scale
        low_ref[rows, :] = (unit * gain).astype(BF16)
        grad_unit = gn_ref[rows, :]
        dy = scale * (grad_unit - unit * head_means(grad_unit * unit, block))
        dy_ref[rows, :] = dy
        q_ref[rows, :] = dot((dy * carried).astype(BF16), cols)
        back_in = dy * grown
        dc_ref[rows, :] = three_dots(back_in, state, NT)
        r_ref[c] = wide_dot(r, back_in, TN)
        return 0

    lax.fori_loop(0, NC, forward, 0, unroll=UNROLL)
    state_ref[...] = r_ref[NC - 1]
    for c in range(NC - 2, -1, -1):
        state_ref[...] = keep_ref[c] * state_ref[...] + r_ref[c]
    pack_payload(pay2, state_ref)
    astern = Exchange(pay2, got2, r3_sems)
    astern.start()
    got2[me] = pay2[me]

    sum_a = PlaneSum(pa, ra_a, ta, rb_a, ha, rc_a, a_sems, True, narrow)
    sum_b = PlaneSum(pb, ra_b, tb, rb_b, hb, rc_b, b_sems, False, narrow_pairs)
    sum_v = PlaneSum(pv, ra_v, tv, rb_v, hv, rc_v, v_sems, True, narrow)
    sum_w = PlaneSum(pw, ra_w, tw, rb_w, hw, rc_w, w_sems, False, narrow)
    deep1 = DepthSum(zs1, zr1, zo1, z1_sems)
    deep2 = DepthSum(zs2, zr2, zo2, z2_sems)

    def spots(m):
        for k in range(4):
            d = 4 * m + k
            yield d >> 3, (d >> 1) & 3, d & 1, slice(32 * k, 32 * k + 32)

    low = low_ref[...]
    for m in range(8):
        gt = g_ref[:, 128 * m:128 * m + 128].T
        out_rows = dot(gt, low).astype(BF16)
        for y, x, core, sub in spots(m):
            pv[core, x, y] = out_rows[sub, 0:512]
            pw[core, y, x] = out_rows[sub, 512:D]
    sum_v.start_pair()
    sum_w.start_pair()
    after = iota((L, L), 1) >= iota((L, L), 0)
    half = iota((2 * L, H), 0) >> 7
    pick = iota((2 * L, H), 1)
    halft = iota((H, 2 * L), 1) >> 7
    pickt = iota((H, 2 * L), 0)

    def inside_backward(c, _):
        rows = chunk_rows(c)
        bc = bc_ref[rows, :]
        b, r = bc[:, 0:N], bc[:, N:2 * N]
        running = run_ref[rows, :]
        runt = runt_ref[c]
        dy_low = dy_ref[rows, :].astype(BF16)
        scaled = sc_ref[rows, :].astype(BF16)
        scores_t = wide_dot(b, r, NT)
        dscores_t = jnp.zeros((L, L), F32)
        by_source = jnp.zeros((L, H), F32)
        by_target = jnp.zeros((H, L), F32)
        for j in range(H // 2):
            pair = slice(128 * j, 128 * j + 128)
            sp = scaled[:, pair]
            dp = dy_low[:, pair]
            zero = jnp.zeros_like(sp)
            mixes, flows = [], []
            for e in (0, 1):
                h = 2 * j + e
                spread = runt[h:h + 1, :] - running[:, h:h + 1]
                decay = jnp.exp(jnp.where(after, spread, -jnp.inf))
                mixes.append((decay * scores_t).astype(BF16))
                mine = jnp.where(even, sp, zero) if e == 0 else jnp.where(even, zero, sp)
                moved = dot(mine, dp, NT) * decay
                dscores_t = dscores_t + moved
                flows.append((moved * scores_t).astype(BF16))
            stacked = jnp.concatenate(
                [jnp.where(even, dp, zero), jnp.where(even, zero, dp)], axis=0
            )
            yin_ref[rows, pair] = dot(jnp.concatenate(mixes, axis=1), stacked)
            which = (pick == 2 * j + half).astype(F32).astype(BF16)
            which_t = (pickt == 2 * j + halft).astype(F32).astype(BF16)
            by_source = by_source + dot(jnp.concatenate(flows, axis=1), which)
            by_target = by_target + dot(which_t, jnp.concatenate(flows, axis=0))
        db_ref[rows, :] = three_dots(dscores_t, r)
        dc_ref[rows, :] = dc_ref[rows, :] + three_dots(dscores_t, b, TN)
        q_ref[rows, :] = q_ref[rows, :] + (by_target.T - by_source)
        return 0

    lax.fori_loop(0, 2, inside_backward, 0)
    astern.wait()
    relay_prefix(got2, mid2, got1, True)
    astern_back = Exchange(mid2, ent2, r4_sems)
    astern_back.start()
    ent2[me] = mid2[me]
    sum_v.start_first()
    sum_w.start_first()
    lax.fori_loop(2, NC, inside_backward, 0)
    sum_v.start_second()
    sum_w.start_second()
    astern_back.wait()
    unpack_state(ent2, u_ref.at[NC - 1])
    for c in range(NC - 1, 0, -1):
        u_ref[c - 1] = keep_ref[c] * u_ref[c] + r_ref[c]

    def backward(c, _):
        rows = chunk_rows(c)
        grad = u_ref[c]
        fade = fade_ref[rows, :]
        weighted = sc_ref[rows, :] * fade
        d_weighted = wide_dot(bc_ref[rows, 0:N], grad)
        used = dot((d_weighted * weighted).astype(BF16), cols)
        db = db_ref[rows, :] + three_dots(weighted, grad, NT)
        held = keep_ref[c] * jnp.sum(grad * s_ref[c], axis=0, keepdims=True)
        held = dot_exact_right(jnp.broadcast_to(held, (8, D)), cols)[0:1]
        d_scaled = d_weighted * fade + yin_ref[rows, :]
        d_running = q_ref[rows, :] - used
        d_last = jnp.sum(used, axis=0, keepdims=True) + held
        d_decay = dot_exact_left3(upper, d_running) + d_last
        direct = dot((d_scaled * v_ref[rows, :]).astype(BF16), cols)
        gd = ((direct - rate * d_decay) * sigmoid(raw_ref[rows, :])).astype(BF16)
        gd_ref[rows, :] = gd
        gp_ref[rows, 0:D] = (d_scaled * wid_ref[rows, :] + skip * dy_ref[rows, :]).astype(BF16)
        gp_ref[rows, D:PROJ] = jnp.concatenate([db, dc_ref[rows, :]], axis=1).astype(BF16)
        gs = dot(gp_ref[rows, :], wpt[...]) + dot(gd, wd[...])
        tok[pl.ds(c * (L // BLK), L // BLK)] = gs.astype(BF16).reshape(L // BLK, BLK, D)
        return 0

    lax.fori_loop(0, NC, backward, 0, unroll=UNROLL)
    gp = gp_ref[...]
    gd = gd_ref[...]
    for m in range(8):
        xt = xt_ref[128 * m:128 * m + 128, :]
        rows_p = dot(xt, gp)
        rows_d = dot(xt, gd)
        dt_hi, dt_lo = split2(rows_d)
        rows_p = rows_p.astype(BF16)
        rows_d = jnp.concatenate([dt_hi, dt_lo, jnp.zeros((128, 128 - 2 * H), BF16)], axis=1)
        for y, x, core, sub in spots(m):
            pa[core, x, y] = rows_p[sub, 0:HALF]
            pb[core, y, x, :, 0:PROJ - HALF] = rows_p[sub, HALF:PROJ]
            pb[core, y, x, :, PROJ - HALF:HALF] = rows_d[sub]
    sum_a.start_pair()
    sum_b.start_pair()

    def send_back(d, _):
        ret[d] = tok[inv_ref[0, d]]
        return 0

    lax.fori_loop(0, NSEQ, send_back, 0, unroll=4)
    grads_back = Exchange(ret, back, lv_sems)
    grads_back.start(1, SPLIT)
    back[me] = ret[me]
    sum_a.start_first()
    sum_b.start_first()
    grads_back.start(SPLIT, NSEQ)
    for k, plane in enumerate((sum_v, sum_w)):
        sum_rows = plane.finish()
        for i in range(4):
            zs2[4 * k + i] = sum_rows[8 * i:8 * i + 8]
    deep2.start()
    sum_a.start_second()
    sum_b.start_second()
    deep2.spread()
    for k, plane in enumerate((sum_a, sum_b)):
        sum_rows = plane.finish()
        for i in range(4):
            zs1[4 * k + i] = sum_rows[8 * i:8 * i + 8]
    deep1.start()
    deep2.finish()
    deep1.spread()
    grads_back.wait()
    deep1.finish()


def place_kernel(src_ref, back_ref, zo1_ref, zo2_ref, out_ref, gp_ref, gd_ref, go_ref):
    def settle(j, _):
        out_ref[src_ref[0, j]] = back_ref[j]
        return 0

    lax.fori_loop(0, NSEQ, settle, 0, unroll=4)
    tails = []
    for i in range(4):
        rows = slice(8 * i, 8 * i + 8)
        for k in range(2):
            go_ref[rows, 512 * k:512 * k + 512] = zo2_ref[4 * k + i]
        gp_ref[rows, 0:HALF] = zo1_ref[i]
        gp_ref[rows, HALF:PROJ] = zo1_ref[4 + i, :, 0:PROJ - HALF]
        tails.append(zo1_ref[4 + i, :, PROJ - HALF:HALF])
    turned = jnp.concatenate(tails, axis=0).T
    gd_ref[...] = turned[0:H] + turned[H:2 * H]


def local(tokens, grad_out, src_order, dst_order, w_proj, w_dt, w_out,
          dt_bias, decay_rate, d_skip, norm_gain):
    blocks = (NSEQ, BLK, D)
    vm = pltpu.VMEM
    dma = pltpu.SemaphoreType.DMA
    block = vm(blocks, BF16)
    full = vm((T, D), F32)
    low = vm((T, D), BF16)
    states = vm((NC, N, D), F32)
    pay, piece = vm((NSEQ, 8, 384), F32), vm((NSEQ, 8, 256), F32)

    def plane(width):
        line = vm((4, 32, width), BF16)
        square = vm((4, 4, 32, width), BF16)
        return [vm((2, 4, 4, 32, width), BF16), square, square, square, line, line]

    scratch = (
        [block, block, vm((D, PROJ), BF16), vm((H, D), BF16), vm((D, D), BF16),
         vm((PROJ, D), BF16), vm((D, D), BF16), vm((D, T), BF16)]
        + [block] * 4 + [low] * 2
        + [full, vm((T, 2 * N), F32), vm((T, H), F32), vm((T, H), F32), vm((NC, H, L), F32)]
        + [states] + [full] * 3
        + [pay, pay] + [piece] * 6
        + [full, full, full, low, vm((T, H), F32), vm((T, N), F32), vm((T, N), F32)]
        + [states, states]
        + [vm((N, D), F32), vm((NC, 1, D), F32), vm((T, PROJ), BF16), vm((T, H), BF16), block]
        + [pltpu.SMEM((1, NSEQ), jnp.int32)]
        + plane(HALF) + plane(HALF) + plane(512) + plane(512)
        + [vm((NDP, 8, HALF), F32)] * 2 + [vm((NDP, 8, 512), F32)] * 2
        + [dma((5,))] + [dma((2,))] * 7 + [dma((6,))] * 4 + [dma((4,))] * 2
    )
    hbm = pl.BlockSpec(memory_space=pl.ANY)
    back, zo1, zo2 = pl.pallas_call(
        whole_kernel,
        out_shape=[
            jax.ShapeDtypeStruct(blocks, BF16),
            jax.ShapeDtypeStruct((NDP, 8, HALF), F32),
            jax.ShapeDtypeStruct((NDP, 8, 512), F32),
        ],
        in_specs=[SM] * 2 + [hbm] * 5 + [VM] * 4,
        out_specs=[VM] * 3,
        scratch_shapes=scratch,
        compiler_params=pltpu.CompilerParams(
            collective_id=0, has_side_effects=True, vmem_limit_bytes=VMEM_LIMIT
        ),
        name="whole",
    )(
        src_order, dst_order,
        tokens.reshape(blocks), grad_out.reshape(blocks), w_proj, w_dt.T, w_out,
        dt_bias.reshape(1, H), decay_rate.reshape(1, H), d_skip.reshape(1, H),
        norm_gain.reshape(1, D),
    )
    grad_tokens, gp, gd, go = pl.pallas_call(
        place_kernel,
        out_shape=[
            jax.ShapeDtypeStruct(blocks, BF16),
            jax.ShapeDtypeStruct((32, PROJ), F32),
            jax.ShapeDtypeStruct((H, 32), F32),
            jax.ShapeDtypeStruct((32, D), F32),
        ],
        in_specs=[SM] + [VM] * 3,
        out_specs=[VM] * 4,
        compiler_params=pltpu.CompilerParams(vmem_limit_bytes=VMEM_LIMIT),
        name="place",
    )(src_order, back, zo1, zo2)
    return grad_tokens.reshape(1, T, D), gp, gd.T, go.T


def solution(mesh):
    in_specs = (
        P("dp", "seq", None), P("dp", "seq", None), P("seq", None), P("seq", None),
        P(), P(), P(), P(), P(), P(), P(),
    )
    out_specs = (P("dp", "seq", None), P("seq", None), P("seq", None), P(None, "seq"))
    return jax.shard_map(local, mesh=mesh, in_specs=in_specs, out_specs=out_specs, check_vma=False)
```

```python
import functools

import jax
import jax.numpy as jnp
from jax import lax
from jax.experimental import pallas as pl
from jax.experimental.pallas import tpu as pltpu
from jax.sharding import PartitionSpec as P

H = 16
P_SIZE = 64
N = 64
D = 1024
PROJ = 1152
BLK = 16
NSEQ = 32
NDP = 8
T = 512
L = 128
NC = T // L
EPSILON = 1e-05
F32 = jnp.float32
BF16 = jnp.bfloat16
MESH = pl.DeviceIdType.MESH
VMEM_LIMIT = 62 * 1024 * 1024
HALF = 640
SPLIT = 32
UNROLL = 2
LATER = 1

VM = pl.BlockSpec(memory_space=pltpu.VMEM)
SM = pl.BlockSpec(memory_space=pltpu.SMEM)

NN = (((1,), (0,)), ((), ()))
NT = (((1,), (1,)), ((), ()))
TN = (((0,), (0,)), ((), ()))


def dot(a, b, dims=NN):
    return lax.dot_general(a, b, dims, preferred_element_type=F32)


def split2(a):
    hi = a.astype(BF16)
    return hi, (a - hi.astype(F32)).astype(BF16)


def split3(a):
    hi, mid = split2(a)
    low = a - hi.astype(F32) - mid.astype(F32)
    return hi, mid, low.astype(BF16)


def dot_exact_right(a, b, dims=NN):
    hi, lo = split2(a)
    return dot(hi, b, dims) + dot(lo, b, dims)


def dot_exact_left3(a, b):
    hi, mid, low = split3(b)
    return (dot(a, low) + dot(a, mid)) + dot(a, hi)


def wide_dot(a, b, dims=NN):
    ka, kb = dims[0][0][0], dims[0][1][0]
    ah, al = split2(a)
    bh, bl = split2(b)
    return dot(
        jnp.concatenate([ah, al, ah], axis=ka), jnp.concatenate([bh, bh, bl], axis=kb), dims
    )


def three_dots(a, b, dims=NN):
    ah, al = split2(a)
    bh, bl = split2(b)
    return (dot(al, bh, dims) + dot(ah, bl, dims)) + dot(ah, bh, dims)


def expand(a, heads2):
    return dot(jnp.concatenate(split2(a), axis=1), heads2)


def thrice(a, axis, second):
    hi, lo = split2(a)
    return jnp.concatenate([hi, hi, lo] if second else [hi, lo, hi], axis=axis)


def head_means(a, block):
    low = a.astype(BF16)
    return jnp.concatenate(
        [dot(low[:, 128 * j:128 * j + 128], block) for j in range(8)], axis=1
    ) * (1.0 / P_SIZE)


def iota(shape, dim):
    return lax.broadcasted_iota(jnp.int32, shape, dim)


def head_rows():
    return ((iota((H, D), 1) >> 6) == iota((H, D), 0)).astype(F32).astype(BF16)


def head_columns():
    return ((iota((D, H), 0) >> 6) == iota((D, H), 1)).astype(F32).astype(BF16)


def lower_ones():
    return (iota((L, L), 0) >= iota((L, L), 1)).astype(F32).astype(BF16)


def upper_ones():
    return (iota((L, L), 0) <= iota((L, L), 1)).astype(F32).astype(BF16)


def softplus(v):
    return jnp.maximum(v, 0.0) + jnp.log1p(jnp.exp(-jnp.abs(v)))


def sigmoid(v):
    e = jnp.exp(-jnp.abs(v))
    return jnp.where(v >= 0, 1.0, e) / (1.0 + e)


def pack_payload(pay_ref, state_ref, keep=None):
    for rg in range(8):
        for lg in range(4):
            lanes = slice(256 * lg, 256 * lg + 256)
            pay_ref[rg * 4 + lg, :, 0:256] = state_ref[8 * rg:8 * rg + 8, lanes]
            if keep is not None:
                first = keep[:, 256 * lg:256 * lg + 128]
                second = keep[:, 256 * lg + 128:256 * lg + 256]
                row = iota((8, 128), 0)
                pay_ref[rg * 4 + lg, :, 256:384] = jnp.where(row == 0, first, second)


def unpack_state(ref, state_ref):
    for rg in range(8):
        for lg in range(4):
            state_ref[8 * rg:8 * rg + 8, 256 * lg:256 * lg + 256] = ref[rg * 4 + lg]


def to_peer(src, dst, send_sem, recv_sem, peer):
    return pltpu.make_async_remote_copy(
        src_ref=src, dst_ref=dst, send_sem=send_sem, recv_sem=recv_sem,
        device_id=peer, device_id_type=MESH,
    )


def places():
    z = lax.axis_index("dp")
    me = lax.axis_index("seq")
    return z, me // 8, lax.rem(me // 2, 4), lax.rem(me, 2)


def greet():
    z = lax.axis_index("dp")
    me = lax.axis_index("seq")
    barrier = pltpu.get_barrier_semaphore()

    def hello(k, _):
        pl.semaphore_signal(
            barrier, inc=1, device_id=(z, lax.rem(me + k, NSEQ)), device_id_type=MESH
        )
        return 0

    def hello_z(k, _):
        pl.semaphore_signal(
            barrier, inc=1, device_id=(lax.rem(z + k, NDP), me), device_id_type=MESH
        )
        return 0

    for k in range(1, NSEQ):
        hello(k, 0)
    for k in range(1, NDP):
        hello_z(k, 0)


def greeted():
    pl.semaphore_wait(pltpu.get_barrier_semaphore(), NSEQ - 1 + NDP - 1)


class Exchange:
    def __init__(self, send, recv, sems):
        self.send, self.recv = send, recv
        self.ss, self.rs = sems.at[0], sems.at[1]

    def start(self, first=1, last=NSEQ):
        z = lax.axis_index("dp")
        me = lax.axis_index("seq")
        for k in range(first, last):
            to = lax.rem(me + k, NSEQ)
            to_peer(self.send.at[to], self.recv.at[me], self.ss, self.rs, (z, to)).start()

    def wait(self):
        z = lax.axis_index("dp")
        me = lax.axis_index("seq")
        most = pl.ds(0, NSEQ - 1)
        copy = to_peer(self.send.at[most], self.recv.at[most], self.ss, self.rs,
                       (z, lax.rem(me + 1, NSEQ)))
        copy.wait_send()
        copy.wait_recv()


def narrow(total):
    return total.astype(BF16)


def narrow_pairs(total):
    start = total.shape[1] - 128
    tail = total[:, start:]
    high = tail.astype(BF16).astype(F32)
    rest = (tail - high)[:, 0:H]
    moved = jnp.concatenate(
        [jnp.zeros_like(rest), rest, jnp.zeros((rest.shape[0], 128 - 2 * H), F32)], axis=1
    )
    lane = iota(tail.shape, 1)
    tail = jnp.where(lane < H, high, tail + moved)
    return jnp.concatenate([total[:, 0:start], tail], axis=1).astype(BF16)


class PlaneSum:
    def __init__(self, part, ra, t, rb, h, rc, sems, x_first, form):
        self.part, self.ra, self.t, self.rb, self.h, self.rc = part, ra, t, rb, h, rc
        self.sems, self.form = sems, form
        z, y, x, core = places()
        self.core = core
        at_x = lambda k: (z, 8 * y + 2 * lax.rem(x + k, 4) + core)
        at_y = lambda k: (z, 8 * lax.rem(y + k, 4) + 2 * x + core)
        self.first = (x, at_x) if x_first else (y, at_y)
        self.second = (y, at_y) if x_first else (x, at_x)
        partner = (z, 8 * y + 2 * x + 1 - core)
        self.pair = to_peer(part.at[1 - core], ra, sems.at[0], sems.at[1], partner)

    def hop(self, src, dst, where, sem):
        here, place = where
        for k in (1, 2, 3):
            to_peer(src.at[lax.rem(here + k, 4)], dst.at[here],
                    self.sems.at[sem], self.sems.at[sem + 1], place(k)).start()

    def hopped(self, src, dst, where, sem):
        here, place = where
        most = pl.ds(0, 3)
        copy = to_peer(src.at[most], dst.at[most], self.sems.at[sem], self.sems.at[sem + 1],
                       place(1))
        copy.wait_send()
        copy.wait_recv()

    def start_pair(self):
        self.pair.start()

    def start_first(self):
        self.pair.wait()

        def body(i, _):
            a, b = i // 4, lax.rem(i, 4)
            self.t[a, b] = self.form(
                self.part[self.core, a, b].astype(F32) + self.ra[a, b].astype(F32)
            )
            return 0

        lax.fori_loop(0, 16, body, 0)
        self.hop(self.t, self.rb, self.first, 2)

    def start_second(self):
        self.hopped(self.t, self.rb, self.first, 2)
        here = self.first[0]

        def body(b, _):
            total = self.t[here, b].astype(F32)
            for k in (1, 2, 3):
                total = total + self.rb[lax.rem(here + k, 4), b].astype(F32)
            self.h[b] = self.form(total)
            return 0

        lax.fori_loop(0, 4, body, 0)
        self.hop(self.h, self.rc, self.second, 4)

    def finish(self):
        self.hopped(self.h, self.rc, self.second, 4)
        here = self.second[0]
        total = self.h[here].astype(F32)
        for k in (1, 2, 3):
            total = total + self.rc[lax.rem(here + k, 4)].astype(F32)
        return total


class DepthSum:
    def __init__(self, zs, zr, zo, sems):
        self.zs, self.zr, self.zo, self.sems = zs, zr, zo, sems
        self.z = lax.axis_index("dp")
        self.me = lax.axis_index("seq")

    def out(self, source, target, sem):
        for k in range(1, NDP):
            to = lax.rem(self.z + k, NDP)
            to_peer(source(to), target, self.sems.at[sem], self.sems.at[sem + 1],
                    (to, self.me)).start()

    def done(self, src, dst, sem):
        most = pl.ds(0, NDP - 1)
        copy = to_peer(src.at[most], dst.at[most], self.sems.at[sem], self.sems.at[sem + 1],
                       (lax.rem(self.z + 1, NDP), self.me))
        copy.wait_send()
        copy.wait_recv()

    def start(self):
        self.out(lambda to: self.zs.at[to], self.zr.at[self.z], 0)

    def spread(self):
        self.done(self.zs, self.zr, 0)

        total = self.zs[self.z]
        for k in range(1, NDP):
            total = total + self.zr[lax.rem(self.z + k, NDP)]
        self.zo[self.z] = total * ((NDP * NSEQ * T) ** (-0.5))
        self.out(lambda to: self.zo.at[self.z], self.zo.at[self.z], 2)

    def finish(self):
        self.done(self.zo, self.zo, 2)


def relay_prefix(recv, mid, keeps, reverse):
    def step(i, state):
        j = NSEQ - 1 - i if reverse else i
        mid[j] = state
        keep = jnp.concatenate([keeps[j, 0:1, 256:384], keeps[j, 1:2, 256:384]], axis=1)
        return keep * state + recv[j, :, 0:256]

    lax.fori_loop(0, NSEQ, step, jnp.zeros((8, 256), F32), unroll=4)


def chunk_rows(c):
    return pl.ds(pl.multiple_of(c * L, L), L)


def keep_row(last, heads):
    return dot_exact_right(jnp.broadcast_to(jnp.exp(last), (8, H)), heads)[0:1]


def keep_row3(total, heads):
    hi, mid, low = split3(jnp.broadcast_to(jnp.exp(total), (8, H)))
    return ((dot(low, heads) + dot(mid, heads)) + dot(hi, heads))[0:1]


def whole_kernel(
    src_ref, dst_ref, tok_hbm, grad_hbm, wp_hbm, wd_hbm, wo_hbm,
    bias_ref, rate_ref, skip_ref, gain_ref,
    back_hbm, zo1, zo2,
    tok, grd, wp, wd, wo, wpt, wot, xt_ref, send_t, send_g, recv_t, recv_g, x_ref, g_ref,
    v_ref, bc_ref, raw_ref, run_ref, runt_ref, u_ref, sc_ref, wid_ref, fade_ref,
    pay1, got1, mid1, ent1, pay2, got2, mid2, ent2,
    yin_ref, gn_ref, dy_ref, low_ref, q_ref, dc_ref, db_ref, s_ref, r_ref,
    state_ref, keep_ref, gp_ref, gd_ref, ret, back, inv_ref,
    pa, ra_a, ta, rb_a, ha, rc_a, pb, ra_b, tb, rb_b, hb, rc_b,
    pv, ra_v, tv, rb_v, hv, rc_v, pw, ra_w, tw, rb_w, hw, rc_w,
    zs1, zr1, zs2, zr2,
    load_sems, st_sems, sg_sems, r1_sems, r2_sems, r3_sems, r4_sems, lv_sems,
    a_sems, b_sems, v_sems, w_sems, z1_sems, z2_sems,
):
    me = lax.axis_index("seq")
    loads = [
        pltpu.make_async_copy(a, b, load_sems.at[i])
        for i, (a, b) in enumerate(
            [(tok_hbm, tok), (grad_hbm, grd), (wp_hbm, wp), (wd_hbm, wd), (wo_hbm, wo)]
        )
    ]
    loads[0].start()
    greet()
    loads[1].start()
    tokens_in = Exchange(send_t, recv_t, st_sems)
    grads_in = Exchange(send_g, recv_g, sg_sems)
    loads[0].wait()

    def load_t(d, _):
        send_t[d] = tok[src_ref[0, d]]
        return 0

    def load_g(d, _):
        send_g[d] = grd[src_ref[0, d]]
        return 0

    def invert(s, _):
        place = 0
        for j in range(NSEQ):
            place = jnp.where(dst_ref[0, j] == s, j, place)
        inv_ref[0, s] = place
        return 0

    lax.fori_loop(0, NSEQ, load_t, 0, unroll=4)
    loads[1].wait()
    lax.fori_loop(0, NSEQ, load_g, 0, unroll=4)
    for load in loads[2:]:
        load.start()
    lax.fori_loop(0, NSEQ, invert, 0)
    greeted()
    tokens_in.start()
    grads_in.start(1, SPLIT)
    recv_t[me] = send_t[me]
    recv_g[me] = send_g[me]

    heads = head_rows()
    cols = head_columns()
    lower = lower_ones()
    upper = upper_ones()
    even = iota((1, 128), 1) < 64
    heads2 = jnp.concatenate([heads, heads], axis=0)
    block = ((iota((128, 128), 0) >> 6) == (iota((128, 128), 1) >> 6)).astype(F32).astype(BF16)
    bias = bias_ref[...]
    rate = rate_ref[...]
    gain = gain_ref[...]
    skip = dot_exact_right(jnp.broadcast_to(skip_ref[...], (8, H)), heads)[0:1]
    loads[2].wait()
    loads[3].wait()
    loads[4].wait()
    wpt[...] = wp[...].T
    wot[...] = wo[...].T
    tokens_in.wait()

    def settle_t(j, _):
        x_ref[pl.ds(pl.multiple_of(j * BLK, BLK), BLK), :] = recv_t[dst_ref[0, j]]
        return 0

    lax.fori_loop(0, NSEQ, settle_t, 0, unroll=4)

    def project(c, total):
        rows = chunk_rows(c)
        x = x_ref[rows, :]
        v = dot(x, wp[:, 0:D])
        v_ref[rows, :] = v
        bc = dot(x, wp[:, D:PROJ])
        bc_ref[rows, :] = bc
        raw = dot(x, wd[...], NT) + bias
        raw_ref[rows, :] = raw
        delta = softplus(raw)
        running = dot_exact_left3(lower, -rate * delta)
        run_ref[rows, :] = running
        runt_ref[c] = running.T
        last = running[L - 1:L, :]
        keep_ref[c] = keep_row(last, heads)
        widened = expand(delta, heads2)
        wid_ref[rows, :] = widened
        scaled = v * widened
        sc_ref[rows, :] = scaled
        fade = expand(jnp.exp(last - running), heads2)
        fade_ref[rows, :] = fade
        u_ref[c] = wide_dot(bc[:, 0:N], scaled * fade, TN)
        return total + last

    total = lax.fori_loop(0, NC, project, jnp.zeros((1, H), F32), unroll=UNROLL)
    keep_all = keep_row3(total, heads)
    state_ref[...] = u_ref[0]
    for c in range(1, NC):
        state_ref[...] = keep_ref[c] * state_ref[...] + u_ref[c]
    pack_payload(pay1, state_ref, keep_all)
    ahead = Exchange(pay1, got1, r1_sems)
    ahead.start()
    grads_in.start(SPLIT, NSEQ)
    got1[me] = pay1[me]
    xt_ref[...] = x_ref[...].T

    below = iota((L, L), 0) >= iota((L, L), 1)

    def inside_forward(c, _):
        rows = chunk_rows(c)
        bc = bc_ref[rows, :]
        running = run_ref[rows, :]
        runt = runt_ref[c]
        scores = wide_dot(bc[:, N:2 * N], bc[:, 0:N], NT)
        scaled = sc_ref[rows, :].astype(BF16)
        for j in range(H // 2):
            mixes = []
            for h in (2 * j, 2 * j + 1):
                spread = running[:, h:h + 1] - runt[h:h + 1, :]
                decay = jnp.exp(jnp.where(below, spread, -jnp.inf))
                mixes.append((decay * scores).astype(BF16))
            pair = scaled[:, 128 * j:128 * j + 128]
            zero = jnp.zeros_like(pair)
            stacked = jnp.concatenate(
                [jnp.where(even, pair, zero), jnp.where(even, zero, pair)], axis=0
            )
            yin_ref[rows, 128 * j:128 * j + 128] = dot(jnp.concatenate(mixes, axis=1), stacked)
        return 0

    lax.fori_loop(0, 3, inside_forward, 0)
    ahead.wait()
    relay_prefix(got1, mid1, got1, False)
    ahead_back = Exchange(mid1, ent1, r2_sems)
    ahead_back.start()
    ent1[me] = mid1[me]
    lax.fori_loop(3, NC, inside_forward, 0)
    grads_in.wait()

    def settle_g(j, _):
        g_ref[pl.ds(pl.multiple_of(j * BLK, BLK), BLK), :] = recv_g[dst_ref[0, j]]
        return 0

    lax.fori_loop(0, NSEQ, settle_g, 0, unroll=4)

    def project_grads(c, _):
        rows = chunk_rows(c)
        gn_ref[rows, :] = dot(g_ref[rows, :], wot[...]) * gain
        return 0

    lax.fori_loop(0, NC, project_grads, 0)
    ahead_back.wait()
    unpack_state(ent1, s_ref.at[0])
    for c in range(1, NC):
        s_ref[c] = keep_ref[c - 1] * s_ref[c - 1] + u_ref[c - 1]

    def forward(c, _):
        rows = chunk_rows(c)
        r = bc_ref[rows, N:2 * N]
        state = s_ref[c]
        grown = expand(jnp.exp(run_ref[rows, :]), heads2)
        carried = wide_dot(r, state) * grown
        summed = yin_ref[rows, :] + carried + skip * v_ref[rows, :]
        scale = lax.rsqrt(head_means(summed * summed, block) + EPSILON)
        unit = summed * scale
        low_ref[rows, :] = (unit * gain).astype(BF16)
        grad_unit = gn_ref[rows, :]
        dy = scale * (grad_unit - unit * head_means(grad_unit * unit, block))
        dy_ref[rows, :] = dy
        q_ref[rows, :] = dot((dy * carried).astype(BF16), cols)
        back_in = dy * grown
        dc_ref[rows, :] = three_dots(back_in, state, NT)
        r_ref[c] = wide_dot(r, back_in, TN)
        return 0

    lax.fori_loop(0, NC, forward, 0, unroll=UNROLL)
    state_ref[...] = r_ref[NC - 1]
    for c in range(NC - 2, -1, -1):
        state_ref[...] = keep_ref[c] * state_ref[...] + r_ref[c]
    pack_payload(pay2, state_ref)
    astern = Exchange(pay2, got2, r3_sems)
    astern.start()
    got2[me] = pay2[me]

    sum_a = PlaneSum(pa, ra_a, ta, rb_a, ha, rc_a, a_sems, True, narrow)
    sum_b = PlaneSum(pb, ra_b, tb, rb_b, hb, rc_b, b_sems, False, narrow_pairs)
    sum_v = PlaneSum(pv, ra_v, tv, rb_v, hv, rc_v, v_sems, True, narrow)
    sum_w = PlaneSum(pw, ra_w, tw, rb_w, hw, rc_w, w_sems, False, narrow)
    deep1 = DepthSum(zs1, zr1, zo1, z1_sems)
    deep2 = DepthSum(zs2, zr2, zo2, z2_sems)

    def spots(m):
        for k in range(4):
            d = 4 * m + k
            yield d >> 3, (d >> 1) & 3, d & 1, slice(32 * k, 32 * k + 32)

    low = low_ref[...]
    for m in range(8):
        gt = g_ref[:, 128 * m:128 * m + 128].T
        out_rows = dot(gt, low).astype(BF16)
        for y, x, core, sub in spots(m):
            pv[core, x, y] = out_rows[sub, 0:512]
            pw[core, y, x] = out_rows[sub, 512:D]
    sum_v.start_pair()
    sum_w.start_pair()
    after = iota((L, L), 1) >= iota((L, L), 0)
    half = iota((2 * L, H), 0) >> 7
    pick = iota((2 * L, H), 1)
    halft = iota((H, 2 * L), 1) >> 7
    pickt = iota((H, 2 * L), 0)

    def inside_backward(c, _):
        rows = chunk_rows(c)
        bc = bc_ref[rows, :]
        b, r = bc[:, 0:N], bc[:, N:2 * N]
        running = run_ref[rows, :]
        runt = runt_ref[c]
        dy_low = dy_ref[rows, :].astype(BF16)
        scaled = sc_ref[rows, :].astype(BF16)
        scores_t = wide_dot(b, r, NT)
        dscores_t = jnp.zeros((L, L), F32)
        by_source = jnp.zeros((L, H), F32)
        by_target = jnp.zeros((H, L), F32)
        for j in range(H // 2):
            pair = slice(128 * j, 128 * j + 128)
            sp = scaled[:, pair]
            dp = dy_low[:, pair]
            zero = jnp.zeros_like(sp)
            mixes, flows = [], []
            for e in (0, 1):
                h = 2 * j + e
                spread = runt[h:h + 1, :] - running[:, h:h + 1]
                decay = jnp.exp(jnp.where(after, spread, -jnp.inf))
                mixes.append((decay * scores_t).astype(BF16))
                mine = jnp.where(even, sp, zero) if e == 0 else jnp.where(even, zero, sp)
                moved = dot(mine, dp, NT) * decay
                dscores_t = dscores_t + moved
                flows.append((moved * scores_t).astype(BF16))
            stacked = jnp.concatenate(
                [jnp.where(even, dp, zero), jnp.where(even, zero, dp)], axis=0
            )
            yin_ref[rows, pair] = dot(jnp.concatenate(mixes, axis=1), stacked)
            which = (pick == 2 * j + half).astype(F32).astype(BF16)
            which_t = (pickt == 2 * j + halft).astype(F32).astype(BF16)
            by_source = by_source + dot(jnp.concatenate(flows, axis=1), which)
            by_target = by_target + dot(which_t, jnp.concatenate(flows, axis=0))
        db_ref[rows, :] = three_dots(dscores_t, r)
        dc_ref[rows, :] = dc_ref[rows, :] + three_dots(dscores_t, b, TN)
        q_ref[rows, :] = q_ref[rows, :] + (by_target.T - by_source)
        return 0

    lax.fori_loop(0, 2, inside_backward, 0)
    astern.wait()
    relay_prefix(got2, mid2, got1, True)
    astern_back = Exchange(mid2, ent2, r4_sems)
    astern_back.start()
    ent2[me] = mid2[me]
    sum_v.start_first()
    sum_w.start_first()
    lax.fori_loop(2, NC, inside_backward, 0)
    sum_v.start_second()
    sum_w.start_second()
    astern_back.wait()
    unpack_state(ent2, u_ref.at[NC - 1])
    for c in range(NC - 1, 0, -1):
        u_ref[c - 1] = keep_ref[c] * u_ref[c] + r_ref[c]

    def backward(c, _):
        rows = chunk_rows(c)
        grad = u_ref[c]
        fade = fade_ref[rows, :]
        weighted = sc_ref[rows, :] * fade
        d_weighted = wide_dot(bc_ref[rows, 0:N], grad)
        used = dot((d_weighted * weighted).astype(BF16), cols)
        db = db_ref[rows, :] + three_dots(weighted, grad, NT)
        held = keep_ref[c] * jnp.sum(grad * s_ref[c], axis=0, keepdims=True)
        held = dot_exact_right(jnp.broadcast_to(held, (8, D)), cols)[0:1]
        d_scaled = d_weighted * fade + yin_ref[rows, :]
        d_running = q_ref[rows, :] - used
        d_last = jnp.sum(used, axis=0, keepdims=True) + held
        d_decay = dot_exact_left3(upper, d_running) + d_last
        direct = dot((d_scaled * v_ref[rows, :]).astype(BF16), cols)
        gd = ((direct - rate * d_decay) * sigmoid(raw_ref[rows, :])).astype(BF16)
        gd_ref[rows, :] = gd
        gp_ref[rows, 0:D] = (d_scaled * wid_ref[rows, :] + skip * dy_ref[rows, :]).astype(BF16)
        gp_ref[rows, D:PROJ] = jnp.concatenate([db, dc_ref[rows, :]], axis=1).astype(BF16)
        gs = dot(gp_ref[rows, :], wpt[...]) + dot(gd, wd[...])
        tok[pl.ds(c * (L // BLK), L // BLK)] = gs.astype(BF16).reshape(L // BLK, BLK, D)
        return 0

    lax.fori_loop(0, NC, backward, 0, unroll=UNROLL)
    gp = gp_ref[:, 0:HALF]
    for m in range(8):
        rows_p = dot(xt_ref[128 * m:128 * m + 128, :], gp).astype(BF16)
        for y, x, core, sub in spots(m):
            pa[core, x, y] = rows_p[sub]
    sum_a.start_pair()
    gp = gp_ref[:, HALF:PROJ]
    gd = gd_ref[...]
    for m in range(8):
        xt = xt_ref[128 * m:128 * m + 128, :]
        rows_p = dot(xt, gp).astype(BF16)
        dt_hi, dt_lo = split2(dot(xt, gd))
        rows_d = jnp.concatenate([dt_hi, dt_lo, jnp.zeros((128, 128 - 2 * H), BF16)], axis=1)
        for y, x, core, sub in spots(m):
            pb[core, y, x, :, 0:PROJ - HALF] = rows_p[sub]
            pb[core, y, x, :, PROJ - HALF:HALF] = rows_d[sub]
    sum_b.start_pair()

    def send_back(d, _):
        ret[d] = tok[inv_ref[0, d]]
        return 0

    lax.fori_loop(0, NSEQ, send_back, 0, unroll=4)
    grads_back = Exchange(ret, back, lv_sems)
    grads_back.start(1, LATER)
    back[me] = ret[me]
    sum_a.start_first()
    sum_b.start_first()
    for k, plane in enumerate((sum_v, sum_w)):
        sum_rows = plane.finish()
        for i in range(4):
            zs2[4 * k + i] = sum_rows[8 * i:8 * i + 8]
    deep2.start()
    sum_a.start_second()
    sum_b.start_second()
    grads_back.start(LATER, NSEQ)
    deep2.spread()
    for k, plane in enumerate((sum_a, sum_b)):
        sum_rows = plane.finish()
        for i in range(4):
            zs1[4 * k + i] = sum_rows[8 * i:8 * i + 8]
    deep1.start()
    deep2.finish()
    deep1.spread()
    grads_back.wait()
    keep_back = pltpu.make_async_copy(back, back_hbm, load_sems.at[5])
    keep_back.start()
    deep1.finish()
    keep_back.wait()


def place_kernel(src_ref, back_ref, zo1_ref, zo2_ref, out_ref, gp_ref, gd_ref, go_ref):
    def settle(j, _):
        out_ref[src_ref[0, j]] = back_ref[j]
        return 0

    lax.fori_loop(0, NSEQ, settle, 0, unroll=4)
    tails = []
    for i in range(4):
        rows = slice(8 * i, 8 * i + 8)
        for k in range(2):
            go_ref[rows, 512 * k:512 * k + 512] = zo2_ref[4 * k + i]
        gp_ref[rows, 0:HALF] = zo1_ref[i]
        gp_ref[rows, HALF:PROJ] = zo1_ref[4 + i, :, 0:PROJ - HALF]
        tails.append(zo1_ref[4 + i, :, PROJ - HALF:HALF])
    turned = jnp.concatenate(tails, axis=0).T
    gd_ref[...] = turned[0:H] + turned[H:2 * H]


def local(tokens, grad_out, src_order, dst_order, w_proj, w_dt, w_out,
          dt_bias, decay_rate, d_skip, norm_gain):
    blocks = (NSEQ, BLK, D)
    vm = pltpu.VMEM
    dma = pltpu.SemaphoreType.DMA
    block = vm(blocks, BF16)
    full = vm((T, D), F32)
    low = vm((T, D), BF16)
    states = vm((NC, N, D), F32)
    pay, piece = vm((NSEQ, 8, 384), F32), vm((NSEQ, 8, 256), F32)

    def plane(width):
        line = vm((4, 32, width), BF16)
        square = vm((4, 4, 32, width), BF16)
        return [vm((2, 4, 4, 32, width), BF16), square, square, square, line, line]

    scratch = (
        [block, block, vm((D, PROJ), BF16), vm((H, D), BF16), vm((D, D), BF16),
         vm((PROJ, D), BF16), vm((D, D), BF16), vm((D, T), BF16)]
        + [block] * 4 + [low] * 2
        + [full, vm((T, 2 * N), F32), vm((T, H), F32), vm((T, H), F32), vm((NC, H, L), F32)]
        + [states] + [full] * 3
        + [pay, pay] + [piece] * 6
        + [full, full, full, low, vm((T, H), F32), vm((T, N), F32), vm((T, N), F32)]
        + [states, states]
        + [vm((N, D), F32), vm((NC, 1, D), F32), vm((T, PROJ), BF16), vm((T, H), BF16), block, block]
        + [pltpu.SMEM((1, NSEQ), jnp.int32)]
        + plane(HALF) + plane(HALF) + plane(512) + plane(512)
        + [vm((NDP, 8, HALF), F32)] * 2 + [vm((NDP, 8, 512), F32)] * 2
        + [dma((6,))] + [dma((2,))] * 7 + [dma((6,))] * 4 + [dma((4,))] * 2
    )
    hbm = pl.BlockSpec(memory_space=pl.ANY)
    back, zo1, zo2 = pl.pallas_call(
        whole_kernel,
        out_shape=[
            jax.ShapeDtypeStruct(blocks, BF16),
            jax.ShapeDtypeStruct((NDP, 8, HALF), F32),
            jax.ShapeDtypeStruct((NDP, 8, 512), F32),
        ],
        in_specs=[SM] * 2 + [hbm] * 5 + [VM] * 4,
        out_specs=[hbm, VM, VM],
        scratch_shapes=scratch,
        compiler_params=pltpu.CompilerParams(
            collective_id=0, has_side_effects=True, vmem_limit_bytes=VMEM_LIMIT
        ),
        name="whole",
    )(
        src_order, dst_order,
        tokens.reshape(blocks), grad_out.reshape(blocks), w_proj, w_dt.T, w_out,
        dt_bias.reshape(1, H), decay_rate.reshape(1, H), d_skip.reshape(1, H),
        norm_gain.reshape(1, D),
    )
    grad_tokens, gp, gd, go = pl.pallas_call(
        place_kernel,
        out_shape=[
            jax.ShapeDtypeStruct(blocks, BF16),
            jax.ShapeDtypeStruct((32, PROJ), F32),
            jax.ShapeDtypeStruct((H, 32), F32),
            jax.ShapeDtypeStruct((32, D), F32),
        ],
        in_specs=[SM] + [VM] * 3,
        out_specs=[VM] * 4,
        compiler_params=pltpu.CompilerParams(vmem_limit_bytes=VMEM_LIMIT),
        name="place",
    )(src_order, back, zo1, zo2)
    return grad_tokens.reshape(1, T, D), gp, gd.T, go.T


def solution(mesh):
    in_specs = (
        P("dp", "seq", None), P("dp", "seq", None), P("seq", None), P("seq", None),
        P(), P(), P(), P(), P(), P(), P(),
    )
    out_specs = (P("dp", "seq", None), P("seq", None), P("seq", None), P(None, "seq"))
    return jax.shard_map(local, mesh=mesh, in_specs=in_specs, out_specs=out_specs, check_vma=False)
```
